32 devices in a mesh: mode: 8 (over y, x, core), wave: 4 (over z).
Axes of the slice: x: 2, y: 2, z: 4, core: 2. Of those that a mesh axis runs over, the one named last changes fastest.
Arguments:
- field_in: bfloat16 [4, 8, 2, 512, 512], P('wave', 'mode'), may hold values from -6 to 6
- target: bfloat16 [4, 8, 2, 512, 512], P('wave', 'mode'), may hold values from -6 to 6
- mask_old: bfloat16 [2, 512, 512], replicated, may hold values from -1 to 1
- scales: float32 [4], P('wave'), may hold values from 0.5 to 2
Outputs:
- mask_one: bfloat16 [2, 512, 512], P(None, 'mode')
- mask_two: bfloat16 [2, 512, 512], P(None, 'mode')
The draws below stay inside these ranges and needn't reach their ends.
All inputs are finite; a program needn't handle non-finite values.
Results may differ from the reference program's by a relative error of at most 0.013.
Values may be sent and summed in bfloat16 or wider, within the bound.
A program may use at most 64 MiB of HBM per device.

```python
import math
import jax
import jax.numpy as jnp
from jax import lax

PIXELS = 512
MODES = 8
WAVES = 4


def steps_of(own_key, extent, cuts, least, largest):
    def one(position, blocks):
        heights = jax.random.uniform(jax.random.fold_in(jax.random.fold_in(own_key, 6), position), (blocks,), jnp.float32, least / len(cuts), largest / len(cuts))
        return jnp.repeat(jnp.exp(heights), extent[position] // blocks).reshape((-1,) + (1,) * (len(extent) - position - 1))

    level = one(*cuts[0])
    for cut in cuts[1:]:
        level = level * one(*cut)
    return level


def noise(stream_key, shape, spread, bound, cuts=(), kind=jnp.bfloat16):
    entries = jax.random.normal(stream_key, shape, jnp.float32) * spread
    if len(cuts) > 0:
        entries = steps_of(stream_key, shape, cuts, -0.22, 0.18) * entries
    return jnp.clip(entries, min=-bound, max=bound).astype(kind)


def setup_inputs(seed: int = 0) -> dict:
    keys = jax.random.split(jax.random.key(seed), 5)
    return {
        "field_in": noise(keys[0], (WAVES, MODES, 2, PIXELS, PIXELS), 1.0, 6.0, ((0, 4), (1, 8))),
        "target": noise(keys[1], (WAVES, MODES, 2, PIXELS, PIXELS), 1.0, 6.0, ((0, 4), (1, 8))),
        "mask_old": jnp.clip(jax.random.uniform(keys[2], (2, PIXELS, PIXELS), jnp.float32, -1.0, 1.0), -1.0, 1.0).astype(jnp.bfloat16),
        "scales": jnp.clip(jnp.exp(math.log(2.0) - 1.3862944 * jax.random.uniform(keys[3], (WAVES,), jnp.float32) ** steps_of(keys[3], (WAVES,), ((0, 4),), -0.2, 0.2)), 0.5, 2.0),
    }


def chirp(scale, count):
    pos = jnp.arange(count, dtype=jnp.float32)
    diff = pos[:, None] - pos[None, :]
    angle = jnp.pi * scale * diff * diff / count
    factor = jnp.float32(count) ** (-0.5)
    return ((jnp.cos(angle) * factor).astype(jnp.bfloat16), (jnp.sin(angle) * factor).astype(jnp.bfloat16))

def right_matrix(real_part, imag_part, sign):
    upper = jnp.concatenate([real_part, sign * imag_part], 1)
    lower = jnp.concatenate([-sign * imag_part, real_part], 1)
    return jnp.concatenate([upper, lower], 0)

def left_matrix(real_part, imag_part, sign):
    first = jnp.concatenate([real_part, sign * imag_part], 0)
    second = jnp.concatenate([-sign * imag_part, real_part], 0)
    return jnp.stack([first, second], 0)

def propagate(field_re, field_im, real_part, imag_part, sign):
    count = field_re.shape[-1]
    batch = field_re.shape[0]
    joined = jnp.concatenate([field_re, field_im], -1).astype(jnp.float32)
    right = right_matrix(real_part, imag_part, sign).astype(jnp.float32)
    middle = jnp.einsum('brk,kc->brc', joined, right, precision=lax.Precision.HIGHEST).astype(jnp.bfloat16)
    middle = middle.reshape(batch, count, 2, count).astype(jnp.float32)
    left = left_matrix(real_part, imag_part, sign).astype(jnp.float32)
    result = jnp.einsum('pqk,bkpc->bqc', left, middle, precision=lax.Precision.HIGHEST)
    return (result[:, :count], result[:, count:])

def phasor(total):
    count = total.shape[-1] // 2
    power = jnp.sum(total * total) / (count * count)
    real_part = total[:, :count]
    imag_part = total[:, count:]
    factor = lax.rsqrt(real_part * real_part + imag_part * imag_part + power + 1e-06)
    return jnp.stack([real_part * factor, imag_part * factor], 0).astype(jnp.bfloat16)

def reference(field_in, target, mask_old, scales):
    old_re = mask_old[0].astype(jnp.float32)
    old_im = mask_old[1].astype(jnp.float32)

    def backward(carry, items):
        fields, targets, scale = items
        kernel_re, kernel_im = chirp(scale, PIXELS)
        f_re = fields[:, 0].astype(jnp.float32)
        f_im = fields[:, 1].astype(jnp.float32)
        b_re = targets[:, 0].astype(jnp.float32)
        b_im = targets[:, 1].astype(jnp.float32)
        c_re = (b_re * old_re + b_im * old_im).astype(jnp.bfloat16)
        c_im = (b_im * old_re - b_re * old_im).astype(jnp.bfloat16)
        back_re, back_im = propagate(c_re, c_im, kernel_re, kernel_im, -1.0)
        term = jnp.concatenate([lax.optimization_barrier(jnp.sum(back_re * f_re + back_im * f_im, 0)), lax.optimization_barrier(jnp.sum(back_im * f_re - back_re * f_im, 0))], -1)
        return (carry + term, None)
    start = jnp.zeros((PIXELS, 2 * PIXELS), jnp.float32)
    margin_one, unused = lax.scan(backward, start, (field_in, target, scales))
    mask_one = phasor(margin_one)
    new_re = mask_one[0].astype(jnp.float32)
    new_im = mask_one[1].astype(jnp.float32)

    def forward(carry, items):
        fields, targets, scale = items
        kernel_re, kernel_im = chirp(scale, PIXELS)
        f_re = fields[:, 0].astype(jnp.float32)
        f_im = fields[:, 1].astype(jnp.float32)
        b_re = targets[:, 0].astype(jnp.float32)
        b_im = targets[:, 1].astype(jnp.float32)
        g_re = (f_re * new_re - f_im * new_im).astype(jnp.bfloat16)
        g_im = (f_re * new_im + f_im * new_re).astype(jnp.bfloat16)
        ahead_re, ahead_im = propagate(g_re, g_im, kernel_re, kernel_im, 1.0)
        term = jnp.concatenate([lax.optimization_barrier(jnp.sum(b_re * ahead_re + b_im * ahead_im, 0)), lax.optimization_barrier(jnp.sum(b_im * ahead_re - b_re * ahead_im, 0))], -1)
        return (carry + term, None)
    margin_two, unused = lax.scan(forward, start, (field_in, target, scales))
    mask_two = phasor(margin_two)
    return (mask_one, mask_two)
```

```python
import functools

import jax
import jax.numpy as jnp
from jax import lax
from jax.experimental import pallas as pl
from jax.experimental.pallas import tpu as pltpu
from jax.sharding import PartitionSpec as P

MESH = pl.DeviceIdType.MESH
F32 = jnp.float32
BF16 = jnp.bfloat16
SUB = 16
LANES = 128


def build_right(scale, right, count):
    wide = 2 * count
    row = lax.broadcasted_iota(jnp.int32, (SUB, wide), 0)
    col = lax.broadcasted_iota(jnp.int32, (SUB, wide), 1)
    diff = (row - col + count).astype(F32)
    angle = (jnp.pi * scale) * diff * diff / count
    factor = float(count) ** (-0.5)
    base_re = jnp.cos(angle) * factor
    base_im = jnp.sin(angle) * factor
    for shift in range(0, LANES, SUB):
        re = (pltpu.roll(base_re, shift, 1) if shift else base_re).astype(BF16)
        im = (pltpu.roll(base_im, shift, 1) if shift else base_im).astype(BF16)
        for hop in range(count // LANES):
            top = hop * LANES + shift
            begin = count - hop * LANES
            k_re = re[:, begin : begin + count]
            k_im = im[:, begin : begin + count]
            right[pl.ds(top, SUB), pl.ds(0, count)] = k_re
            right[pl.ds(top, SUB), pl.ds(count, count)] = k_im
            right[pl.ds(count + top, SUB), pl.ds(0, count)] = -k_im
            right[pl.ds(count + top, SUB), pl.ds(count, count)] = k_re


def kernel(
    modes,
    waves,
    scale_ref,
    field,
    target,
    old,
    out_one,
    out_two,
    right,
    joined,
    middle,
    part,
    core_in,
    chip_out,
    chip_in,
    wave_out,
    wave_in,
    whole,
    last,
    power_out,
    power_in,
    power_out2,
    power_in2,
    core_s,
    core_r,
    chip_s,
    chip_r,
    wave_s,
    wave_r,
    gw_s,
    gw_r,
    gx_s,
    gx_r,
    gc_s,
    gc_r,
    pm_s,
    pm_r,
    pw_s,
    pw_r,
):
    count = field.shape[-1]
    chips = modes // 2
    rows = count // modes
    piece = rows // waves
    mode = lax.axis_index("mode")
    wave = lax.axis_index("wave")
    core = lax.rem(mode, 2)
    chip = lax.div(mode, 2)
    other = 1 - core

    barrier = pltpu.get_barrier_semaphore()
    for step in range(1, modes):
        pl.semaphore_signal(
            barrier, inc=1, device_id={"mode": lax.rem(mode + step, modes)}, device_id_type=MESH
        )
    for step in range(1, waves):
        pl.semaphore_signal(
            barrier, inc=1, device_id={"wave": lax.rem(wave + step, waves)}, device_id_type=MESH
        )

    def send(src, dst, s_sem, r_sem, to):
        copy = pltpu.make_async_remote_copy(
            src_ref=src, dst_ref=dst, send_sem=s_sem, recv_sem=r_sem, device_id=to, device_id_type=MESH
        )
        copy.start()
        return copy

    pending = []

    def right_product():
        for half, low in ((0, count), (1, 0)):
            middle[pl.ds(low, count), :] = jnp.dot(
                joined[...], right[:, pl.ds(half * count, count)], preferred_element_type=F32
            ).astype(BF16)

    def left_half(which, term):
        starts = [pl.multiple_of((2 * q + which) * rows, rows) for q in range(chips)]
        lhs = jnp.concatenate(
            [right[pl.ds(s, rows), :] for s in starts]
            + [right[pl.ds(pl.multiple_of(count + s, rows), rows), :] for s in starts],
            0,
        )
        result = jnp.dot(lhs, middle[...], preferred_element_type=F32)
        for q in range(chips):
            im = result[q * rows : (q + 1) * rows]
            re = result[(chips + q) * rows : (chips + q + 1) * rows]
            at = pl.ds(starts[q], rows)
            term_re, term_im = term(re, im, at)
            part[which, q, :, pl.ds(0, count)] = term_re.astype(BF16)
            part[which, q, :, pl.ds(count, count)] = term_im.astype(BF16)

    def reduce_scatter(trip, term, ready):
        left_half(other, term)
        ready()
        crossing = send(
            part.at[other], core_in.at[trip], core_s.at[trip], core_r.at[trip], {"mode": 2 * chip + other}
        )
        left_half(core, term)
        crossing.wait_recv()
        copies = []
        for step in range(1, chips):
            to = lax.rem(chip + step, chips)
            chip_out[trip, step] = (
                part[core, to].astype(F32) + core_in[trip, to].astype(F32)
            ).astype(BF16)
            copies.append(
                send(
                    chip_out.at[trip, step],
                    chip_in.at[trip, step],
                    chip_s.at[trip, step],
                    chip_r.at[trip, step],
                    {"mode": 2 * to + core},
                )
            )
        total = part[core, chip].astype(F32) + core_in[trip, chip].astype(F32)
        for step, copy in enumerate(copies, 1):
            copy.wait_recv()
            total = total + chip_in[trip, step].astype(F32)
        wave_out[trip] = total.astype(BF16).reshape(waves, piece, 2 * count)
        hops = []
        for step in range(1, waves):
            to = lax.rem(wave + step, waves)
            hops.append(
                send(
                    wave_out.at[trip, to],
                    wave_in.at[trip, step],
                    wave_s.at[trip, step],
                    wave_r.at[trip, step],
                    {"wave": to},
                )
            )
        result = wave_out[trip, wave].astype(F32)
        for step, copy in enumerate(hops, 1):
            copy.wait_recv()
            result = result + wave_in[trip, step].astype(F32)
        pending.extend([crossing] + copies + hops)
        return result

    def phasor(block, power):
        re = block[:, :count]
        im = block[:, count:]
        factor = lax.rsqrt(re * re + im * im + power + 1e-06)
        return (re * factor).astype(BF16), (im * factor).astype(BF16)

    build_right(scale_ref[0], right, count)

    t_re = target[0].astype(F32)
    t_im = target[1].astype(F32)
    o_re = old[0].astype(F32)
    o_im = old[1].astype(F32)
    joined[:, pl.ds(0, count)] = (t_re * o_re + t_im * o_im).astype(BF16)
    joined[:, pl.ds(count, count)] = (t_re * o_im - t_im * o_re).astype(BF16)
    right_product()

    def term_one(re, im, at):
        f_re = field[0, at, :].astype(F32)
        f_im = field[1, at, :].astype(F32)
        return re * f_re - im * f_im, -(re * f_im + im * f_re)

    def entered():
        pl.semaphore_wait(barrier, modes - 1 + waves - 1)

    margin = reduce_scatter(0, term_one, entered)

    at = pl.ds(pl.multiple_of(wave * piece, piece), piece)
    whole[core, chip, at, :] = margin.astype(BF16)
    own = whole.at[core, chip, at]
    hops = [
        send(own, own, gw_s.at[step], gw_r.at[step], {"wave": lax.rem(wave + step, waves)})
        for step in range(1, waves)
    ]
    for copy in hops:
        copy.wait_recv()
    block = whole.at[core, chip]
    fans = [
        send(block, block, gx_s.at[step], gx_r.at[step], {"mode": 2 * lax.rem(chip + step, chips) + core})
        for step in range(1, chips)
    ]
    across = [send(block, block, gc_s.at[0], gc_r.at[0], {"mode": 2 * chip + other})]
    for step, copy in enumerate(fans, 1):
        copy.wait_recv()
        came = whole.at[core, lax.rem(chip - step + chips, chips)]
        across.append(send(came, came, gc_s.at[step], gc_r.at[step], {"mode": 2 * chip + other}))
    for copy in across:
        copy.wait_recv()
    pending.extend(hops + fans + across)

    squares = jnp.zeros((8, 2 * count), F32)
    for c in range(2):
        for q in range(chips):
            block_f = whole[c, q].astype(F32)
            squares = squares + jnp.sum((block_f * block_f).reshape(rows // 8, 8, 2 * count), 0)
    power = jnp.sum(squares, keepdims=True) / (count * count)
    for c in range(2):
        for q in range(chips):
            low = (2 * q + c) * rows
            m_re, m_im = phasor(whole[c, q].astype(F32), power)
            n_re = m_re.astype(F32)
            n_im = m_im.astype(F32)
            f_re = field[0, pl.ds(low, rows), :].astype(F32)
            f_im = field[1, pl.ds(low, rows), :].astype(F32)
            joined[pl.ds(low, rows), pl.ds(0, count)] = (f_re * n_re - f_im * n_im).astype(BF16)
            joined[pl.ds(low, rows), pl.ds(count, count)] = (f_re * n_im + f_im * n_re).astype(BF16)
    right_product()
    m_re, m_im = phasor(whole[core, chip].astype(F32), power)
    out_one[0] = m_re
    out_one[1] = m_im

    def term_two(re, im, at):
        b_re = target[0, at, :].astype(F32)
        b_im = target[1, at, :].astype(F32)
        return b_re * re + b_im * im, b_im * re - b_re * im

    for copy in pending:
        copy.wait_send()
    pending.clear()
    margin = reduce_scatter(1, term_two, lambda: None)
    squares = jnp.sum((margin * margin).reshape(piece // 8, 8, 2 * count), 0)
    tile = squares[:, :LANES]
    for low in range(LANES, 2 * count, LANES):
        tile = tile + squares[:, low : low + LANES]
    power_out[...] = tile
    tiles = [
        send(
            power_out,
            power_in.at[step],
            pm_s.at[step],
            pm_r.at[step],
            {"mode": lax.rem(mode + step, modes)},
        )
        for step in range(1, modes)
    ]
    last[at, :] = margin.astype(BF16)
    own = last.at[at]
    hops = [
        send(own, own, gw_s.at[waves + step], gw_r.at[waves + step], {"wave": lax.rem(wave + step, waves)})
        for step in range(1, waves)
    ]
    for step, copy in enumerate(tiles, 1):
        copy.wait_recv()
        tile = tile + power_in[step]
    power_out2[...] = tile
    tiles2 = [
        send(
            power_out2,
            power_in2.at[step],
            pw_s.at[step],
            pw_r.at[step],
            {"wave": lax.rem(wave + step, waves)},
        )
        for step in range(1, waves)
    ]
    for step, copy in enumerate(tiles2, 1):
        copy.wait_recv()
        tile = tile + power_in2[step]
    power = jnp.sum(tile, keepdims=True) / (count * count)
    for copy in hops:
        copy.wait_recv()
    m_re, m_im = phasor(last[...].astype(F32), power)
    out_two[0] = m_re
    out_two[1] = m_im
    for copy in pending + tiles + hops + tiles2:
        copy.wait_send()


def fused(field_in, target, mask_old, scales):
    modes = lax.axis_size("mode")
    waves = lax.axis_size("wave")
    count = field_in.shape[-1]
    chips = modes // 2
    rows = count // modes
    piece = rows // waves
    dma = pltpu.SemaphoreType.DMA
    out = jax.ShapeDtypeStruct((2, rows, count), BF16)
    vmem = pl.BlockSpec(memory_space=pltpu.VMEM)
    return pl.pallas_call(
        functools.partial(kernel, modes, waves),
        out_shape=(out, out),
        in_specs=[pl.BlockSpec(memory_space=pltpu.SMEM), vmem, vmem, vmem],
        out_specs=(vmem, vmem),
        scratch_shapes=[
            pltpu.VMEM((2 * count, 2 * count), BF16),
            pltpu.VMEM((count, 2 * count), BF16),
            pltpu.VMEM((2 * count, count), BF16),
            pltpu.VMEM((2, chips, rows, 2 * count), BF16),
            pltpu.VMEM((2, chips, rows, 2 * count), BF16),
            pltpu.VMEM((2, chips, rows, 2 * count), BF16),
            pltpu.VMEM((2, chips, rows, 2 * count), BF16),
            pltpu.VMEM((2, waves, piece, 2 * count), BF16),
            pltpu.VMEM((2, waves, piece, 2 * count), BF16),
            pltpu.VMEM((2, chips, rows, 2 * count), BF16),
            pltpu.VMEM((rows, 2 * count), BF16),
            pltpu.VMEM((8, LANES), F32),
            pltpu.VMEM((modes, 8, LANES), F32),
            pltpu.VMEM((8, LANES), F32),
            pltpu.VMEM((waves, 8, LANES), F32),
            dma((2,)),
            dma((2,)),
            dma((2, chips)),
            dma((2, chips)),
            dma((2, waves)),
            dma((2, waves)),
            dma((2 * waves,)),
            dma((2 * waves,)),
            dma((chips,)),
            dma((chips,)),
            dma((chips,)),
            dma((chips,)),
            dma((modes,)),
            dma((modes,)),
            dma((waves,)),
            dma((waves,)),
        ],
        compiler_params=pltpu.CompilerParams(
            collective_id=0, has_side_effects=True, vmem_limit_bytes=48 * 1024 * 1024
        ),
        cost_estimate=pl.CostEstimate(flops=16 * count**3 * 2, bytes_accessed=12 * count**2, transcendentals=0),
    )(scales, field_in[0, 0], target[0, 0], mask_old)


def chirp(scale, count):
    pos = jnp.arange(count, dtype=jnp.float32)
    diff = pos[:, None] - pos[None, :]
    angle = jnp.pi * scale * diff * diff / count
    factor = jnp.float32(count) ** (-0.5)
    return (
        (jnp.cos(angle) * factor).astype(jnp.bfloat16),
        (jnp.sin(angle) * factor).astype(jnp.bfloat16),
    )


def right_matrix(real_part, imag_part, sign):
    upper = jnp.concatenate([real_part, sign * imag_part], 1)
    lower = jnp.concatenate([-sign * imag_part, real_part], 1)
    return jnp.concatenate([upper, lower], 0)


def left_matrix(real_part, imag_part, sign):
    first = jnp.concatenate([real_part, sign * imag_part], 0)
    second = jnp.concatenate([-sign * imag_part, real_part], 0)
    return jnp.stack([first, second], 0)


def right_product(field_re, field_im, right):
    joined = jnp.concatenate([field_re, field_im], -1)
    return jnp.einsum("brk,kc->brc", joined, right, preferred_element_type=jnp.float32).astype(
        jnp.bfloat16
    )


def left_product(middle, left):
    batch = middle.shape[0]
    count = middle.shape[1]
    shaped = middle.reshape(batch, count, 2, count)
    result = jnp.einsum("pqk,bkpc->bqc", left, shaped, preferred_element_type=jnp.float32)
    return (result[:, :count], result[:, count:])


def phasor_rows(total, power_sum, count):
    power = power_sum / (count * count)
    real_part = total[:, :count]
    imag_part = total[:, count:]
    factor = lax.rsqrt(real_part * real_part + imag_part * imag_part + power + 1e-06)
    return jnp.concatenate([real_part * factor, imag_part * factor], -1).astype(jnp.bfloat16)


def as_output(mask_part, count):
    return jnp.stack([mask_part[:, :count], mask_part[:, count:]], 0)


def whole_mask(term):
    total = lax.psum(term, ("mode", "wave"))
    return phasor_rows(total, jnp.sum(total * total), term.shape[1] // 2)


def local(field_in, target, mask_old, scales):
    count = field_in.shape[-1]
    row_count = count // lax.axis_size("mode")
    kernel_re, kernel_im = chirp(scales[0], count)
    f_re = field_in[0, :, 0]
    f_im = field_in[0, :, 1]
    b_re = target[0, :, 0].astype(jnp.float32)
    b_im = target[0, :, 1].astype(jnp.float32)
    old_re = mask_old[0].astype(jnp.float32)
    old_im = mask_old[1].astype(jnp.float32)
    c_re = (b_re * old_re + b_im * old_im).astype(jnp.bfloat16)
    c_im = (b_im * old_re - b_re * old_im).astype(jnp.bfloat16)
    middle = right_product(c_re, c_im, right_matrix(kernel_re, kernel_im, -1.0))
    back_re, back_im = left_product(middle, left_matrix(kernel_re, kernel_im, -1.0))
    fr32 = f_re.astype(jnp.float32)
    fi32 = f_im.astype(jnp.float32)
    term_one = jnp.concatenate(
        [jnp.sum(back_re * fr32 + back_im * fi32, 0), jnp.sum(back_im * fr32 - back_re * fi32, 0)],
        -1,
    )
    forward_right = right_matrix(kernel_re, kernel_im, 1.0)
    mask_full = whole_mask(term_one)
    new_re = mask_full[:, :count].astype(jnp.float32)
    new_im = mask_full[:, count:].astype(jnp.float32)
    g_re = (fr32 * new_re - fi32 * new_im).astype(jnp.bfloat16)
    g_im = (fr32 * new_im + fi32 * new_re).astype(jnp.bfloat16)
    ahead_mid = right_product(g_re, g_im, forward_right)
    first_rows = lax.dynamic_slice_in_dim(
        mask_full, lax.axis_index("mode") * row_count, row_count, 0
    )
    ahead_re, ahead_im = left_product(ahead_mid, left_matrix(kernel_re, kernel_im, 1.0))
    term_two = jnp.concatenate(
        [
            jnp.sum(b_re * ahead_re + b_im * ahead_im, 0),
            jnp.sum(b_im * ahead_re - b_re * ahead_im, 0),
        ],
        -1,
    )
    second_full = whole_mask(term_two)
    second_rows = lax.dynamic_slice_in_dim(
        second_full, lax.axis_index("mode") * row_count, row_count, 0
    )
    return (as_output(first_rows, count), as_output(second_rows, count))


def solution(mesh):
    in_specs = (
        P("wave", "mode", None, None, None),
        P("wave", "mode", None, None, None),
        P(),
        P("wave"),
    )
    out_specs = (P(None, "mode", None), P(None, "mode", None))
    modes, waves = mesh.shape["mode"], mesh.shape["wave"]

    def step(field_in, target, mask_old, scales):
        count = field_in.shape[-1]
        single = field_in.shape[0] == waves and field_in.shape[1] == modes
        fits = modes % 2 == 0 and count % (modes * waves * SUB) == 0 and count % LANES == 0
        body = fused if single and fits else local
        return jax.shard_map(body, mesh=mesh, in_specs=in_specs, out_specs=out_specs, check_vma=False)(
            field_in, target, mask_old, scales
        )

    return step
```

```python
import functools

import jax
import jax.numpy as jnp
from jax import lax
from jax.experimental import pallas as pl
from jax.experimental.pallas import tpu as pltpu
from jax.sharding import PartitionSpec as P

MESH = pl.DeviceIdType.MESH
F32 = jnp.float32
BF16 = jnp.bfloat16
SUB = 16
LANES = 128
CUTS = 2


def build_right(scale, right, count):
    wide = 2 * count
    row = lax.broadcasted_iota(jnp.int32, (SUB, wide), 0)
    col = lax.broadcasted_iota(jnp.int32, (SUB, wide), 1)
    diff = (row - col + count).astype(F32)
    angle = (jnp.pi * scale) * diff * diff / count
    factor = float(count) ** (-0.5)
    base_re = jnp.cos(angle) * factor
    base_im = jnp.sin(angle) * factor
    for shift in range(0, LANES, SUB):
        re = (pltpu.roll(base_re, shift, 1) if shift else base_re).astype(BF16)
        im = (pltpu.roll(base_im, shift, 1) if shift else base_im).astype(BF16)
        for hop in range(count // LANES):
            top = hop * LANES + shift
            begin = count - hop * LANES
            k_re = re[:, begin : begin + count]
            k_im = im[:, begin : begin + count]
            right[pl.ds(top, SUB), pl.ds(0, count)] = k_re
            right[pl.ds(top, SUB), pl.ds(count, count)] = k_im
            right[pl.ds(count + top, SUB), pl.ds(0, count)] = -k_im
            right[pl.ds(count + top, SUB), pl.ds(count, count)] = k_re


def kernel(
    modes,
    waves,
    scale_ref,
    field_hbm,
    target_hbm,
    old_hbm,
    out_one,
    out_two,
    field,
    target,
    old,
    right,
    joined,
    middle,
    part,
    core_in,
    chip_out,
    chip_in,
    wave_out,
    wave_in,
    whole,
    last,
    power_out,
    power_in,
    power_out2,
    power_in2,
    load_s,
    core_s,
    core_r,
    chip_s,
    chip_r,
    wave_s,
    wave_r,
    gw_s,
    gw_r,
    gx_s,
    gx_r,
    gc_s,
    gc_r,
    pm_s,
    pm_r,
    pw_s,
    pw_r,
):
    count = field.shape[-1]
    chips = modes // 2
    rows = count // modes
    piece = rows // waves
    width = count // CUTS
    mode = lax.axis_index("mode")
    wave = lax.axis_index("wave")
    core = lax.rem(mode, 2)
    chip = lax.div(mode, 2)
    other = 1 - core

    loads = [
        pltpu.make_async_copy(src, dst, load_s.at[i])
        for i, (src, dst) in enumerate(((target_hbm, target), (old_hbm, old), (field_hbm, field)))
    ]
    for copy in loads:
        copy.start()

    barrier = pltpu.get_barrier_semaphore()
    for step in range(1, modes):
        pl.semaphore_signal(
            barrier, inc=1, device_id={"mode": lax.rem(mode + step, modes)}, device_id_type=MESH
        )
    for step in range(1, waves):
        pl.semaphore_signal(
            barrier, inc=1, device_id={"wave": lax.rem(wave + step, waves)}, device_id_type=MESH
        )

    pending = []

    def send(src, dst, s_sem, r_sem, to):
        copy = pltpu.make_async_remote_copy(
            src_ref=src, dst_ref=dst, send_sem=s_sem, recv_sem=r_sem, device_id=to, device_id_type=MESH
        )
        copy.start()
        pending.append(copy)
        return copy

    def starts_of(which):
        return [pl.multiple_of((2 * q + which) * rows, rows) for q in range(chips)]

    def right_rows(low, starts):
        size = rows * len(starts)
        for half, base in ((0, count), (1, 0)):
            result = jnp.dot(
                joined[pl.ds(low, size), :],
                right[:, pl.ds(half * count, count)],
                preferred_element_type=F32,
            ).astype(BF16)
            for q, start in enumerate(starts):
                middle[pl.ds(pl.multiple_of(base + start, rows), rows), :] = result[q * rows : (q + 1) * rows]

    def left_half(trip, cut, which, term):
        starts = starts_of(which)
        cols = pl.ds(cut * width, width)
        lhs = jnp.concatenate(
            [right[pl.ds(s, rows), :] for s in starts]
            + [right[pl.ds(pl.multiple_of(count + s, rows), rows), :] for s in starts],
            0,
        )
        result = jnp.dot(lhs, middle[:, cols], preferred_element_type=F32)
        for q in range(chips):
            im = result[q * rows : (q + 1) * rows]
            re = result[(chips + q) * rows : (chips + q + 1) * rows]
            term_re, term_im = term(re, im, pl.ds(starts[q], rows), cols)
            part[trip, cut, which, q, :, pl.ds(0, width)] = term_re.astype(BF16)
            part[trip, cut, which, q, :, pl.ds(width, width)] = term_im.astype(BF16)

    def reduce_scatter(trip, term, ready, arrived):
        fans = []
        for cut in range(CUTS):
            left_half(trip, cut, other, term)
            if cut == 0:
                ready()
            crossing = send(
                part.at[trip, cut, other],
                core_in.at[trip, cut],
                core_s.at[trip, cut],
                core_r.at[trip, cut],
                {"mode": 2 * chip + other},
            )
            left_half(trip, cut, core, term)
            crossing.wait_recv()
            fan = []
            for step in range(1, chips):
                to = lax.rem(chip + step, chips)
                chip_out[trip, cut, step] = (
                    part[trip, cut, core, to].astype(F32) + core_in[trip, cut, to].astype(F32)
                ).astype(BF16)
                fan.append(
                    send(
                        chip_out.at[trip, cut, step],
                        chip_in.at[trip, cut, step],
                        chip_s.at[trip, cut, step],
                        chip_r.at[trip, cut, step],
                        {"mode": 2 * to + core},
                    )
                )
            fans.append(fan)
        hops = []
        for cut in range(CUTS):
            total = part[trip, cut, core, chip].astype(F32) + core_in[trip, cut, chip].astype(F32)
            for step, copy in enumerate(fans[cut], 1):
                copy.wait_recv()
                total = total + chip_in[trip, cut, step].astype(F32)
            wave_out[trip, cut] = total.astype(BF16).reshape(waves, piece, 2 * width)
            hop = []
            for step in range(1, waves):
                to = lax.rem(wave + step, waves)
                hop.append(
                    send(
                        wave_out.at[trip, cut, to],
                        wave_in.at[trip, cut, step],
                        wave_s.at[trip, cut, step],
                        wave_r.at[trip, cut, step],
                        {"wave": to},
                    )
                )
            hops.append(hop)
        for cut in range(CUTS):
            result = wave_out[trip, cut, wave].astype(F32)
            for step, copy in enumerate(hops[cut], 1):
                copy.wait_recv()
                result = result + wave_in[trip, cut, step].astype(F32)
            arrived(cut, result)

    def folded(values):
        squares = jnp.sum((values * values).reshape(piece // 8, 8, 2 * width), 0)
        tile = squares[:, :LANES]
        for low in range(LANES, 2 * width, LANES):
            tile = tile + squares[:, low : low + LANES]
        return tile

    def power_over_modes(trip, tile):
        power_out[trip] = tile
        return [
            send(
                power_out.at[trip],
                power_in.at[trip, step],
                pm_s.at[trip, step],
                pm_r.at[trip, step],
                {"mode": lax.rem(mode + step, modes)},
            )
            for step in range(1, modes)
        ]

    def power_over_waves(trip, tile, copies):
        for step, copy in enumerate(copies, 1):
            copy.wait_recv()
            tile = tile + power_in[trip, step]
        power_out2[trip] = tile
        return tile, [
            send(
                power_out2.at[trip],
                power_in2.at[trip, step],
                pw_s.at[trip, step],
                pw_r.at[trip, step],
                {"wave": lax.rem(wave + step, waves)},
            )
            for step in range(1, waves)
        ]

    def mean_power(trip, tile, copies):
        for step, copy in enumerate(copies, 1):
            copy.wait_recv()
            tile = tile + power_in2[trip, step]
        return jnp.sum(tile, keepdims=True) / (count * count)

    def phasor(block, power):
        re = block[:, :width].astype(F32)
        im = block[:, width:].astype(F32)
        factor = lax.rsqrt(re * re + im * im + power + 1e-06)
        return (re * factor).astype(BF16), (im * factor).astype(BF16)

    build_right(scale_ref[0], right, count)

    loads[0].wait()
    loads[1].wait()
    t_re = target[0].astype(F32)
    t_im = target[1].astype(F32)
    o_re = old[0].astype(F32)
    o_im = old[1].astype(F32)
    joined[:, pl.ds(0, count)] = (t_re * o_re + t_im * o_im).astype(BF16)
    joined[:, pl.ds(count, count)] = (t_re * o_im - t_im * o_re).astype(BF16)
    right_rows(0, [q * rows for q in range(modes)])
    loads[2].wait()

    def term_one(re, im, at, cols):
        f_re = field[0, at, cols].astype(F32)
        f_im = field[1, at, cols].astype(F32)
        return re * f_re - im * f_im, -(re * f_im + im * f_re)

    def entered():
        pl.semaphore_wait(barrier, modes - 1 + waves - 1)

    mine = pl.ds(pl.multiple_of(wave * piece, piece), piece)
    squares = []
    hops = []

    def spread(trip, cut, own, value):
        own[...] = value.astype(BF16)
        hops.append(
            [
                send(
                    own,
                    own,
                    gw_s.at[trip, cut, step],
                    gw_r.at[trip, cut, step],
                    {"wave": lax.rem(wave + step, waves)},
                )
                for step in range(1, waves)
            ]
        )
        squares.append(folded(value))

    reduce_scatter(0, term_one, entered, lambda cut, v: spread(0, cut, whole.at[cut, core, chip, mine], v))
    tile = sum(squares[1:], squares[0])
    tiles = power_over_modes(0, tile)
    fans = []
    across = []
    for cut in range(CUTS):
        for copy in hops[cut]:
            copy.wait_recv()
        block = whole.at[cut, core, chip]
        fans.append(
            [
                send(
                    block,
                    block,
                    gx_s.at[cut, step],
                    gx_r.at[cut, step],
                    {"mode": 2 * lax.rem(chip + step, chips) + core},
                )
                for step in range(1, chips)
            ]
        )
        across.append(send(block, block, gc_s.at[cut, 0], gc_r.at[cut, 0], {"mode": 2 * chip + other}))
    tile, tiles2 = power_over_waves(0, tile, tiles)
    for cut in range(CUTS):
        for step, copy in enumerate(fans[cut], 1):
            copy.wait_recv()
            came = whole.at[cut, core, lax.rem(chip - step + chips, chips)]
            across.append(
                send(came, came, gc_s.at[cut, step], gc_r.at[cut, step], {"mode": 2 * chip + other})
            )
    power = mean_power(0, tile, tiles2)

    def forward_half(which, low):
        starts = starts_of(which)
        for q, start in enumerate(starts):
            at = pl.ds(low + q * rows, rows)
            for cut in range(CUTS):
                cols = pl.ds(cut * width, width)
                m_re, m_im = phasor(whole[cut, which, q], power)
                n_re = m_re.astype(F32)
                n_im = m_im.astype(F32)
                f_re = field[0, pl.ds(start, rows), cols].astype(F32)
                f_im = field[1, pl.ds(start, rows), cols].astype(F32)
                joined[at, cols] = (f_re * n_re - f_im * n_im).astype(BF16)
                joined[at, pl.ds(count + cut * width, width)] = (f_re * n_im + f_im * n_re).astype(BF16)
        right_rows(low, starts)

    forward_half(core, 0)
    for copy in across:
        copy.wait_recv()
    forward_half(other, count // 2)

    def term_two(re, im, at, cols):
        b_re = target[0, at, cols].astype(F32)
        b_im = target[1, at, cols].astype(F32)
        return b_re * re + b_im * im, b_im * re - b_re * im

    squares.clear()
    hops.clear()
    reduce_scatter(1, term_two, lambda: None, lambda cut, v: spread(1, cut, last.at[cut, mine], v))
    tile = sum(squares[1:], squares[0])
    tiles = power_over_modes(1, tile)
    for cut in range(CUTS):
        cols = pl.ds(cut * width, width)
        m_re, m_im = phasor(whole[cut, core, chip], power)
        out_one[0, :, cols] = m_re
        out_one[1, :, cols] = m_im
    tile, tiles2 = power_over_waves(1, tile, tiles)
    for hop in hops:
        for copy in hop:
            copy.wait_recv()
    power = mean_power(1, tile, tiles2)
    for cut in range(CUTS):
        cols = pl.ds(cut * width, width)
        m_re, m_im = phasor(last[cut], power)
        out_two[0, :, cols] = m_re
        out_two[1, :, cols] = m_im
    for copy in pending:
        copy.wait_send()


def fused(field_in, target, mask_old, scales):
    modes = lax.axis_size("mode")
    waves = lax.axis_size("wave")
    count = field_in.shape[-1]
    chips = modes // 2
    rows = count // modes
    piece = rows // waves
    wide = 2 * count // CUTS
    dma = pltpu.SemaphoreType.DMA
    out = jax.ShapeDtypeStruct((2, rows, count), BF16)
    vmem = pl.BlockSpec(memory_space=pltpu.VMEM)
    anywhere = pl.BlockSpec(memory_space=pl.ANY)
    return pl.pallas_call(
        functools.partial(kernel, modes, waves),
        out_shape=(out, out),
        in_specs=[pl.BlockSpec(memory_space=pltpu.SMEM), anywhere, anywhere, anywhere],
        out_specs=(vmem, vmem),
        scratch_shapes=[
            pltpu.VMEM((2, count, count), BF16),
            pltpu.VMEM((2, count, count), BF16),
            pltpu.VMEM((2, count, count), BF16),
            pltpu.VMEM((2 * count, 2 * count), BF16),
            pltpu.VMEM((count, 2 * count), BF16),
            pltpu.VMEM((2 * count, count), BF16),
            pltpu.VMEM((2, CUTS, 2, chips, rows, wide), BF16),
            pltpu.VMEM((2, CUTS, chips, rows, wide), BF16),
            pltpu.VMEM((2, CUTS, chips, rows, wide), BF16),
            pltpu.VMEM((2, CUTS, chips, rows, wide), BF16),
            pltpu.VMEM((2, CUTS, waves, piece, wide), BF16),
            pltpu.VMEM((2, CUTS, waves, piece, wide), BF16),
            pltpu.VMEM((CUTS, 2, chips, rows, wide), BF16),
            pltpu.VMEM((CUTS, rows, wide), BF16),
            pltpu.VMEM((2, 8, LANES), F32),
            pltpu.VMEM((2, modes, 8, LANES), F32),
            pltpu.VMEM((2, 8, LANES), F32),
            pltpu.VMEM((2, waves, 8, LANES), F32),
            dma((3,)),
            dma((2, CUTS)),
            dma((2, CUTS)),
            dma((2, CUTS, chips)),
            dma((2, CUTS, chips)),
            dma((2, CUTS, waves)),
            dma((2, CUTS, waves)),
            dma((2, CUTS, waves)),
            dma((2, CUTS, waves)),
            dma((CUTS, chips)),
            dma((CUTS, chips)),
            dma((CUTS, chips)),
            dma((CUTS, chips)),
            dma((2, modes)),
            dma((2, modes)),
            dma((2, waves)),
            dma((2, waves)),
        ],
        compiler_params=pltpu.CompilerParams(
            collective_id=0, has_side_effects=True, vmem_limit_bytes=56 * 1024 * 1024
        ),
        cost_estimate=pl.CostEstimate(flops=16 * count**3 * 2, bytes_accessed=12 * count**2, transcendentals=0),
    )(scales, field_in[0, 0], target[0, 0], mask_old)


def chirp(scale, count):
    pos = jnp.arange(count, dtype=jnp.float32)
    diff = pos[:, None] - pos[None, :]
    angle = jnp.pi * scale * diff * diff / count
    factor = jnp.float32(count) ** (-0.5)
    return (
        (jnp.cos(angle) * factor).astype(jnp.bfloat16),
        (jnp.sin(angle) * factor).astype(jnp.bfloat16),
    )


def right_matrix(real_part, imag_part, sign):
    upper = jnp.concatenate([real_part, sign * imag_part], 1)
    lower = jnp.concatenate([-sign * imag_part, real_part], 1)
    return jnp.concatenate([upper, lower], 0)


def left_matrix(real_part, imag_part, sign):
    first = jnp.concatenate([real_part, sign * imag_part], 0)
    second = jnp.concatenate([-sign * imag_part, real_part], 0)
    return jnp.stack([first, second], 0)


def right_product(field_re, field_im, right):
    joined = jnp.concatenate([field_re, field_im], -1)
    return jnp.einsum("brk,kc->brc", joined, right, preferred_element_type=jnp.float32).astype(
        jnp.bfloat16
    )


def left_product(middle, left):
    batch = middle.shape[0]
    count = middle.shape[1]
    shaped = middle.reshape(batch, count, 2, count)
    result = jnp.einsum("pqk,bkpc->bqc", left, shaped, preferred_element_type=jnp.float32)
    return (result[:, :count], result[:, count:])


def phasor_rows(total, power_sum, count):
    power = power_sum / (count * count)
    real_part = total[:, :count]
    imag_part = total[:, count:]
    factor = lax.rsqrt(real_part * real_part + imag_part * imag_part + power + 1e-06)
    return jnp.concatenate([real_part * factor, imag_part * factor], -1).astype(jnp.bfloat16)


def as_output(mask_part, count):
    return jnp.stack([mask_part[:, :count], mask_part[:, count:]], 0)


def whole_mask(term):
    total = lax.psum(term, ("mode", "wave"))
    return phasor_rows(total, jnp.sum(total * total), term.shape[1] // 2)


def local(field_in, target, mask_old, scales):
    count = field_in.shape[-1]
    row_count = count // lax.axis_size("mode")
    kernel_re, kernel_im = chirp(scales[0], count)
    f_re = field_in[0, :, 0]
    f_im = field_in[0, :, 1]
    b_re = target[0, :, 0].astype(jnp.float32)
    b_im = target[0, :, 1].astype(jnp.float32)
    old_re = mask_old[0].astype(jnp.float32)
    old_im = mask_old[1].astype(jnp.float32)
    c_re = (b_re * old_re + b_im * old_im).astype(jnp.bfloat16)
    c_im = (b_im * old_re - b_re * old_im).astype(jnp.bfloat16)
    middle = right_product(c_re, c_im, right_matrix(kernel_re, kernel_im, -1.0))
    back_re, back_im = left_product(middle, left_matrix(kernel_re, kernel_im, -1.0))
    fr32 = f_re.astype(jnp.float32)
    fi32 = f_im.astype(jnp.float32)
    term_one = jnp.concatenate(
        [jnp.sum(back_re * fr32 + back_im * fi32, 0), jnp.sum(back_im * fr32 - back_re * fi32, 0)],
        -1,
    )
    forward_right = right_matrix(kernel_re, kernel_im, 1.0)
    mask_full = whole_mask(term_one)
    new_re = mask_full[:, :count].astype(jnp.float32)
    new_im = mask_full[:, count:].astype(jnp.float32)
    g_re = (fr32 * new_re - fi32 * new_im).astype(jnp.bfloat16)
    g_im = (fr32 * new_im + fi32 * new_re).astype(jnp.bfloat16)
    ahead_mid = right_product(g_re, g_im, forward_right)
    first_rows = lax.dynamic_slice_in_dim(
        mask_full, lax.axis_index("mode") * row_count, row_count, 0
    )
    ahead_re, ahead_im = left_product(ahead_mid, left_matrix(kernel_re, kernel_im, 1.0))
    term_two = jnp.concatenate(
        [
            jnp.sum(b_re * ahead_re + b_im * ahead_im, 0),
            jnp.sum(b_im * ahead_re - b_re * ahead_im, 0),
        ],
        -1,
    )
    second_full = whole_mask(term_two)
    second_rows = lax.dynamic_slice_in_dim(
        second_full, lax.axis_index("mode") * row_count, row_count, 0
    )
    return (as_output(first_rows, count), as_output(second_rows, count))


def solution(mesh):
    in_specs = (
        P("wave", "mode", None, None, None),
        P("wave", "mode", None, None, None),
        P(),
        P("wave"),
    )
    out_specs = (P(None, "mode", None), P(None, "mode", None))
    modes, waves = mesh.shape["mode"], mesh.shape["wave"]

    def step(field_in, target, mask_old, scales):
        count = field_in.shape[-1]
        single = field_in.shape[0] == waves and field_in.shape[1] == modes
        fits = modes % 2 == 0 and count % (modes * waves * SUB) == 0 and count % (CUTS * LANES) == 0
        body = fused if single and fits else local
        return jax.shard_map(body, mesh=mesh, in_specs=in_specs, out_specs=out_specs, check_vma=False)(
            field_in, target, mask_old, scales
        )

    return step
```

```python
import functools

import jax
import jax.numpy as jnp
from jax import lax
from jax.experimental import pallas as pl
from jax.experimental.pallas import tpu as pltpu
from jax.sharding import PartitionSpec as P

MESH = pl.DeviceIdType.MESH
F32 = jnp.float32
BF16 = jnp.bfloat16
SUB = 16
LANES = 128
CUTS = 1


def build_right(scale, right, count):
    wide = 2 * count
    half = SUB // 2
    row = lax.broadcasted_iota(jnp.int32, (half, wide), 0)
    col = lax.broadcasted_iota(jnp.int32, (half, wide), 1)
    diff = (row - col + count).astype(F32)
    angle = (jnp.pi * scale) * diff * diff / count
    factor = float(count) ** (-0.5)
    top_re = jnp.cos(angle) * factor
    top_im = jnp.sin(angle) * factor
    base_re = jnp.concatenate([top_re, pltpu.roll(top_re, half, 1)], 0)
    base_im = jnp.concatenate([top_im, pltpu.roll(top_im, half, 1)], 0)
    for shift in range(0, LANES, SUB):
        re = (pltpu.roll(base_re, shift, 1) if shift else base_re).astype(BF16)
        im = (pltpu.roll(base_im, shift, 1) if shift else base_im).astype(BF16)
        for hop in range(count // LANES):
            top = hop * LANES + shift
            begin = count - hop * LANES
            k_re = re[:, begin : begin + count]
            k_im = im[:, begin : begin + count]
            right[pl.ds(top, SUB), pl.ds(0, count)] = k_re
            right[pl.ds(top, SUB), pl.ds(count, count)] = k_im
            right[pl.ds(count + top, SUB), pl.ds(0, count)] = -k_im
            right[pl.ds(count + top, SUB), pl.ds(count, count)] = k_re


def kernel(
    modes,
    waves,
    scale_ref,
    field_hbm,
    target_hbm,
    old_hbm,
    out_one,
    out_two,
    field,
    target,
    old,
    right,
    joined,
    middle,
    part,
    core_in,
    chip_out,
    chip_in,
    wave_out,
    wave_in,
    whole,
    last,
    power_out,
    power_in,
    power_out2,
    power_in2,
    load_s,
    core_s,
    core_r,
    chip_s,
    chip_r,
    wave_s,
    wave_r,
    gw_s,
    gw_r,
    gx_s,
    gx_r,
    gc_s,
    gc_r,
    pm_s,
    pm_r,
    pw_s,
    pw_r,
):
    count = field.shape[-1]
    chips = modes // 2
    rows = count // modes
    piece = rows // waves
    width = count // CUTS
    mode = lax.axis_index("mode")
    wave = lax.axis_index("wave")
    core = lax.rem(mode, 2)
    chip = lax.div(mode, 2)
    other = 1 - core

    loads = [
        pltpu.make_async_copy(src.at[p], dst.at[p], load_s.at[2 * i + p])
        for i, (src, dst) in enumerate(((target_hbm, target), (old_hbm, old), (field_hbm, field)))
        for p in range(2)
    ]
    for copy in loads:
        copy.start()

    barrier = pltpu.get_barrier_semaphore()
    for step in range(1, modes):
        pl.semaphore_signal(
            barrier, inc=1, device_id={"mode": lax.rem(mode + step, modes)}, device_id_type=MESH
        )
    for step in range(1, waves):
        pl.semaphore_signal(
            barrier, inc=1, device_id={"wave": lax.rem(wave + step, waves)}, device_id_type=MESH
        )

    pending = []

    def send(src, dst, s_sem, r_sem, to):
        copy = pltpu.make_async_remote_copy(
            src_ref=src, dst_ref=dst, send_sem=s_sem, recv_sem=r_sem, device_id=to, device_id_type=MESH
        )
        copy.start()
        pending.append(copy)
        return copy

    def starts_of(which):
        return [pl.multiple_of((2 * q + which) * rows, rows) for q in range(chips)]

    def right_rows(low, starts):
        size = rows * len(starts)
        for half, base in ((0, count), (1, 0)):
            result = jnp.dot(
                joined[pl.ds(low, size), :],
                right[:, pl.ds(half * count, count)],
                preferred_element_type=F32,
            ).astype(BF16)
            for q, start in enumerate(starts):
                middle[pl.ds(pl.multiple_of(base + start, rows), rows), :] = result[q * rows : (q + 1) * rows]

    def left_half(trip, cut, which, term):
        starts = starts_of(which)
        cols = pl.ds(cut * width, width)
        lhs = jnp.concatenate(
            [right[pl.ds(s, rows), :] for s in starts]
            + [right[pl.ds(pl.multiple_of(count + s, rows), rows), :] for s in starts],
            0,
        )
        result = jnp.dot(lhs, middle[:, cols], preferred_element_type=F32)
        for q in range(chips):
            im = result[q * rows : (q + 1) * rows]
            re = result[(chips + q) * rows : (chips + q + 1) * rows]
            term_re, term_im = term(re, im, pl.ds(starts[q], rows), cols)
            part[trip, cut, which, q, :, pl.ds(0, width)] = term_re.astype(BF16)
            part[trip, cut, which, q, :, pl.ds(width, width)] = term_im.astype(BF16)

    def reduce_scatter(trip, term, ready, arrived):
        fans = []
        for cut in range(CUTS):
            left_half(trip, cut, other, term)
            if cut == 0:
                ready()
            crossing = send(
                part.at[trip, cut, other],
                core_in.at[trip, cut],
                core_s.at[trip, cut],
                core_r.at[trip, cut],
                {"mode": 2 * chip + other},
            )
            left_half(trip, cut, core, term)
            crossing.wait_recv()
            fan = []
            for step in range(1, chips):
                to = lax.rem(chip + step, chips)
                chip_out[trip, cut, step] = (
                    part[trip, cut, core, to].astype(F32) + core_in[trip, cut, to].astype(F32)
                ).astype(BF16)
                fan.append(
                    send(
                        chip_out.at[trip, cut, step],
                        chip_in.at[trip, cut, step],
                        chip_s.at[trip, cut, step],
                        chip_r.at[trip, cut, step],
                        {"mode": 2 * to + core},
                    )
                )
            fans.append(fan)
        hops = []
        for cut in range(CUTS):
            total = part[trip, cut, core, chip].astype(F32) + core_in[trip, cut, chip].astype(F32)
            for step, copy in enumerate(fans[cut], 1):
                copy.wait_recv()
                total = total + chip_in[trip, cut, step].astype(F32)
            wave_out[trip, cut] = total.astype(BF16).reshape(waves, piece, 2 * width)
            hop = []
            for step in range(1, waves):
                to = lax.rem(wave + step, waves)
                hop.append(
                    send(
                        wave_out.at[trip, cut, to],
                        wave_in.at[trip, cut, step],
                        wave_s.at[trip, cut, step],
                        wave_r.at[trip, cut, step],
                        {"wave": to},
                    )
                )
            hops.append(hop)
        for cut in range(CUTS):
            result = wave_out[trip, cut, wave].astype(F32)
            for step, copy in enumerate(hops[cut], 1):
                copy.wait_recv()
                result = result + wave_in[trip, cut, step].astype(F32)
            arrived(cut, result)

    def folded(values):
        squares = jnp.sum((values * values).reshape(piece // 8, 8, 2 * width), 0)
        tile = squares[:, :LANES]
        for low in range(LANES, 2 * width, LANES):
            tile = tile + squares[:, low : low + LANES]
        return tile

    def power_over_modes(trip, tile):
        power_out[trip] = tile
        return [
            send(
                power_out.at[trip],
                power_in.at[trip, step],
                pm_s.at[trip, step],
                pm_r.at[trip, step],
                {"mode": lax.rem(mode + step, modes)},
            )
            for step in range(1, modes)
        ]

    def power_over_waves(trip, tile, copies):
        for step, copy in enumerate(copies, 1):
            copy.wait_recv()
            tile = tile + power_in[trip, step]
        power_out2[trip] = tile
        return tile, [
            send(
                power_out2.at[trip],
                power_in2.at[trip, step],
                pw_s.at[trip, step],
                pw_r.at[trip, step],
                {"wave": lax.rem(wave + step, waves)},
            )
            for step in range(1, waves)
        ]

    def mean_power(trip, tile, copies):
        for step, copy in enumerate(copies, 1):
            copy.wait_recv()
            tile = tile + power_in2[trip, step]
        return jnp.sum(tile, keepdims=True) / (count * count)

    def phasor(block, power):
        re = block[:, :width].astype(F32)
        im = block[:, width:].astype(F32)
        factor = lax.rsqrt(re * re + im * im + power + 1e-06)
        return (re * factor).astype(BF16), (im * factor).astype(BF16)

    build_right(scale_ref[0], right, count)

    for copy in loads[:4]:
        copy.wait()
    t_re = target[0].astype(F32)
    t_im = target[1].astype(F32)
    o_re = old[0].astype(F32)
    o_im = old[1].astype(F32)
    joined[:, pl.ds(0, count)] = (t_re * o_re + t_im * o_im).astype(BF16)
    joined[:, pl.ds(count, count)] = (t_re * o_im - t_im * o_re).astype(BF16)
    right_rows(0, [q * rows for q in range(modes)])
    for copy in loads[4:]:
        copy.wait()

    def term_one(re, im, at, cols):
        f_re = field[0, at, cols].astype(F32)
        f_im = field[1, at, cols].astype(F32)
        return re * f_re - im * f_im, -(re * f_im + im * f_re)

    def entered():
        pl.semaphore_wait(barrier, modes - 1 + waves - 1)

    mine = pl.ds(pl.multiple_of(wave * piece, piece), piece)
    squares = []
    hops = []

    def spread(trip, cut, own, value):
        own[...] = value.astype(BF16)
        hops.append(
            [
                send(
                    own,
                    own,
                    gw_s.at[trip, cut, step],
                    gw_r.at[trip, cut, step],
                    {"wave": lax.rem(wave + step, waves)},
                )
                for step in range(1, waves)
            ]
        )
        squares.append(folded(value))

    reduce_scatter(0, term_one, entered, lambda cut, v: spread(0, cut, whole.at[cut, core, chip, mine], v))
    tile = sum(squares[1:], squares[0])
    tiles = power_over_modes(0, tile)
    fans = []
    across = []
    for cut in range(CUTS):
        for copy in hops[cut]:
            copy.wait_recv()
        block = whole.at[cut, core, chip]
        fans.append(
            [
                send(
                    block,
                    block,
                    gx_s.at[cut, step],
                    gx_r.at[cut, step],
                    {"mode": 2 * lax.rem(chip + step, chips) + core},
                )
                for step in range(1, chips)
            ]
        )
        across.append(send(block, block, gc_s.at[cut, 0], gc_r.at[cut, 0], {"mode": 2 * chip + other}))
    tile, tiles2 = power_over_waves(0, tile, tiles)
    for cut in range(CUTS):
        for step, copy in enumerate(fans[cut], 1):
            copy.wait_recv()
            came = whole.at[cut, core, lax.rem(chip - step + chips, chips)]
            across.append(
                send(came, came, gc_s.at[cut, step], gc_r.at[cut, step], {"mode": 2 * chip + other})
            )
    power = mean_power(0, tile, tiles2)

    def forward_half(which, low):
        starts = starts_of(which)
        for q, start in enumerate(starts):
            at = pl.ds(low + q * rows, rows)
            for cut in range(CUTS):
                cols = pl.ds(cut * width, width)
                m_re, m_im = phasor(whole[cut, which, q], power)
                n_re = m_re.astype(F32)
                n_im = m_im.astype(F32)
                f_re = field[0, pl.ds(start, rows), cols].astype(F32)
                f_im = field[1, pl.ds(start, rows), cols].astype(F32)
                joined[at, cols] = (f_re * n_re - f_im * n_im).astype(BF16)
                joined[at, pl.ds(count + cut * width, width)] = (f_re * n_im + f_im * n_re).astype(BF16)
        right_rows(low, starts)

    forward_half(core, 0)
    for copy in across:
        copy.wait_recv()
    forward_half(other, count // 2)

    def term_two(re, im, at, cols):
        b_re = target[0, at, cols].astype(F32)
        b_im = target[1, at, cols].astype(F32)
        return b_re * re + b_im * im, b_im * re - b_re * im

    squares.clear()
    hops.clear()
    reduce_scatter(1, term_two, lambda: None, lambda cut, v: spread(1, cut, last.at[cut, mine], v))
    tile = sum(squares[1:], squares[0])
    tiles = power_over_modes(1, tile)
    for cut in range(CUTS):
        cols = pl.ds(cut * width, width)
        m_re, m_im = phasor(whole[cut, core, chip], power)
        out_one[0, :, cols] = m_re
        out_one[1, :, cols] = m_im
    tile, tiles2 = power_over_waves(1, tile, tiles)
    for hop in hops:
        for copy in hop:
            copy.wait_recv()
    power = mean_power(1, tile, tiles2)
    for cut in range(CUTS):
        cols = pl.ds(cut * width, width)
        m_re, m_im = phasor(last[cut], power)
        out_two[0, :, cols] = m_re
        out_two[1, :, cols] = m_im
    for copy in pending:
        copy.wait_send()


def fused(field_in, target, mask_old, scales):
    modes = lax.axis_size("mode")
    waves = lax.axis_size("wave")
    count = field_in.shape[-1]
    chips = modes // 2
    rows = count // modes
    piece = rows // waves
    wide = 2 * count // CUTS
    dma = pltpu.SemaphoreType.DMA
    out = jax.ShapeDtypeStruct((2, rows, count), BF16)
    vmem = pl.BlockSpec(memory_space=pltpu.VMEM)
    anywhere = pl.BlockSpec(memory_space=pl.ANY)
    return pl.pallas_call(
        functools.partial(kernel, modes, waves),
        out_shape=(out, out),
        in_specs=[pl.BlockSpec(memory_space=pltpu.SMEM), anywhere, anywhere, anywhere],
        out_specs=(vmem, vmem),
        scratch_shapes=[
            pltpu.VMEM((2, count, count), BF16),
            pltpu.VMEM((2, count, count), BF16),
            pltpu.VMEM((2, count, count), BF16),
            pltpu.VMEM((2 * count, 2 * count), BF16),
            pltpu.VMEM((count, 2 * count), BF16),
            pltpu.VMEM((2 * count, count), BF16),
            pltpu.VMEM((2, CUTS, 2, chips, rows, wide), BF16),
            pltpu.VMEM((2, CUTS, chips, rows, wide), BF16),
            pltpu.VMEM((2, CUTS, chips, rows, wide), BF16),
            pltpu.VMEM((2, CUTS, chips, rows, wide), BF16),
            pltpu.VMEM((2, CUTS, waves, piece, wide), BF16),
            pltpu.VMEM((2, CUTS, waves, piece, wide), BF16),
            pltpu.VMEM((CUTS, 2, chips, rows, wide), BF16),
            pltpu.VMEM((CUTS, rows, wide), BF16),
            pltpu.VMEM((2, 8, LANES), F32),
            pltpu.VMEM((2, modes, 8, LANES), F32),
            pltpu.VMEM((2, 8, LANES), F32),
            pltpu.VMEM((2, waves, 8, LANES), F32),
            dma((6,)),
            dma((2, CUTS)),
            dma((2, CUTS)),
            dma((2, CUTS, chips)),
            dma((2, CUTS, chips)),
            dma((2, CUTS, waves)),
            dma((2, CUTS, waves)),
            dma((2, CUTS, waves)),
            dma((2, CUTS, waves)),
            dma((CUTS, chips)),
            dma((CUTS, chips)),
            dma((CUTS, chips)),
            dma((CUTS, chips)),
            dma((2, modes)),
            dma((2, modes)),
            dma((2, waves)),
            dma((2, waves)),
        ],
        compiler_params=pltpu.CompilerParams(
            collective_id=0, has_side_effects=True, vmem_limit_bytes=48 * 1024 * 1024
        ),
        cost_estimate=pl.CostEstimate(flops=16 * count**3 * 2, bytes_accessed=12 * count**2, transcendentals=0),
    )(scales, field_in[0, 0], target[0, 0], mask_old)


def chirp(scale, count):
    pos = jnp.arange(count, dtype=jnp.float32)
    diff = pos[:, None] - pos[None, :]
    angle = jnp.pi * scale * diff * diff / count
    factor = jnp.float32(count) ** (-0.5)
    return (
        (jnp.cos(angle) * factor).astype(jnp.bfloat16),
        (jnp.sin(angle) * factor).astype(jnp.bfloat16),
    )


def right_matrix(real_part, imag_part, sign):
    upper = jnp.concatenate([real_part, sign * imag_part], 1)
    lower = jnp.concatenate([-sign * imag_part, real_part], 1)
    return jnp.concatenate([upper, lower], 0)


def left_matrix(real_part, imag_part, sign):
    first = jnp.concatenate([real_part, sign * imag_part], 0)
    second = jnp.concatenate([-sign * imag_part, real_part], 0)
    return jnp.stack([first, second], 0)


def right_product(field_re, field_im, right):
    joined = jnp.concatenate([field_re, field_im], -1)
    return jnp.einsum("brk,kc->brc", joined, right, preferred_element_type=jnp.float32).astype(
        jnp.bfloat16
    )


def left_product(middle, left):
    batch = middle.shape[0]
    count = middle.shape[1]
    shaped = middle.reshape(batch, count, 2, count)
    result = jnp.einsum("pqk,bkpc->bqc", left, shaped, preferred_element_type=jnp.float32)
    return (result[:, :count], result[:, count:])


def phasor_rows(total, power_sum, count):
    power = power_sum / (count * count)
    real_part = total[:, :count]
    imag_part = total[:, count:]
    factor = lax.rsqrt(real_part * real_part + imag_part * imag_part + power + 1e-06)
    return jnp.concatenate([real_part * factor, imag_part * factor], -1).astype(jnp.bfloat16)


def as_output(mask_part, count):
    return jnp.stack([mask_part[:, :count], mask_part[:, count:]], 0)


def whole_mask(term):
    total = lax.psum(term, ("mode", "wave"))
    return phasor_rows(total, jnp.sum(total * total), term.shape[1] // 2)


def local(field_in, target, mask_old, scales):
    count = field_in.shape[-1]
    row_count = count // lax.axis_size("mode")
    kernel_re, kernel_im = chirp(scales[0], count)
    f_re = field_in[0, :, 0]
    f_im = field_in[0, :, 1]
    b_re = target[0, :, 0].astype(jnp.float32)
    b_im = target[0, :, 1].astype(jnp.float32)
    old_re = mask_old[0].astype(jnp.float32)
    old_im = mask_old[1].astype(jnp.float32)
    c_re = (b_re * old_re + b_im * old_im).astype(jnp.bfloat16)
    c_im = (b_im * old_re - b_re * old_im).astype(jnp.bfloat16)
    middle = right_product(c_re, c_im, right_matrix(kernel_re, kernel_im, -1.0))
    back_re, back_im = left_product(middle, left_matrix(kernel_re, kernel_im, -1.0))
    fr32 = f_re.astype(jnp.float32)
    fi32 = f_im.astype(jnp.float32)
    term_one = jnp.concatenate(
        [jnp.sum(back_re * fr32 + back_im * fi32, 0), jnp.sum(back_im * fr32 - back_re * fi32, 0)],
        -1,
    )
    forward_right = right_matrix(kernel_re, kernel_im, 1.0)
    mask_full = whole_mask(term_one)
    new_re = mask_full[:, :count].astype(jnp.float32)
    new_im = mask_full[:, count:].astype(jnp.float32)
    g_re = (fr32 * new_re - fi32 * new_im).astype(jnp.bfloat16)
    g_im = (fr32 * new_im + fi32 * new_re).astype(jnp.bfloat16)
    ahead_mid = right_product(g_re, g_im, forward_right)
    first_rows = lax.dynamic_slice_in_dim(
        mask_full, lax.axis_index("mode") * row_count, row_count, 0
    )
    ahead_re, ahead_im = left_product(ahead_mid, left_matrix(kernel_re, kernel_im, 1.0))
    term_two = jnp.concatenate(
        [
            jnp.sum(b_re * ahead_re + b_im * ahead_im, 0),
            jnp.sum(b_im * ahead_re - b_re * ahead_im, 0),
        ],
        -1,
    )
    second_full = whole_mask(term_two)
    second_rows = lax.dynamic_slice_in_dim(
        second_full, lax.axis_index("mode") * row_count, row_count, 0
    )
    return (as_output(first_rows, count), as_output(second_rows, count))


def solution(mesh):
    in_specs = (
        P("wave", "mode", None, None, None),
        P("wave", "mode", None, None, None),
        P(),
        P("wave"),
    )
    out_specs = (P(None, "mode", None), P(None, "mode", None))
    modes, waves = mesh.shape["mode"], mesh.shape["wave"]

    def step(field_in, target, mask_old, scales):
        count = field_in.shape[-1]
        single = field_in.shape[0] == waves and field_in.shape[1] == modes
        fits = modes % 2 == 0 and count % (modes * waves * SUB) == 0 and count % (CUTS * LANES) == 0
        body = fused if single and fits else local
        return jax.shard_map(body, mesh=mesh, in_specs=in_specs, out_specs=out_specs, check_vma=False)(
            field_in, target, mask_old, scales
        )

    return step
```

```python
import functools

import jax
import jax.numpy as jnp
from jax import lax
from jax.experimental import pallas as pl
from jax.experimental.pallas import tpu as pltpu
from jax.sharding import PartitionSpec as P

MESH = pl.DeviceIdType.MESH
F32 = jnp.float32
BF16 = jnp.bfloat16
SUB = 16
LANES = 128
CUTS = 2


def build_right(scale, right, count):
    wide = 2 * count
    half = SUB // 2
    row = lax.broadcasted_iota(jnp.int32, (half, wide), 0)
    col = lax.broadcasted_iota(jnp.int32, (half, wide), 1)
    diff = (row - col + count).astype(F32)
    angle = (jnp.pi * scale) * diff * diff / count
    factor = float(count) ** (-0.5)
    top_re = jnp.cos(angle) * factor
    top_im = jnp.sin(angle) * factor
    base_re = jnp.concatenate([top_re, pltpu.roll(top_re, half, 1)], 0)
    base_im = jnp.concatenate([top_im, pltpu.roll(top_im, half, 1)], 0)
    for shift in range(0, LANES, SUB):
        re = (pltpu.roll(base_re, shift, 1) if shift else base_re).astype(BF16)
        im = (pltpu.roll(base_im, shift, 1) if shift else base_im).astype(BF16)
        for hop in range(count // LANES):
            top = hop * LANES + shift
            begin = count - hop * LANES
            k_re = re[:, begin : begin + count]
            k_im = im[:, begin : begin + count]
            right[pl.ds(top, SUB), pl.ds(0, count)] = k_re
            right[pl.ds(top, SUB), pl.ds(count, count)] = k_im
            right[pl.ds(count + top, SUB), pl.ds(0, count)] = -k_im
            right[pl.ds(count + top, SUB), pl.ds(count, count)] = k_re


def kernel(
    modes,
    waves,
    scale_ref,
    field_hbm,
    target_hbm,
    old_hbm,
    masks,
    field,
    target,
    old,
    right,
    joined,
    middle,
    part,
    core_in,
    chip_out,
    chip_in,
    wave_out,
    wave_in,
    whole,
    last,
    power_out,
    power_in,
    power_out2,
    power_in2,
    load_s,
    core_s,
    core_r,
    chip_s,
    chip_r,
    wave_s,
    wave_r,
    gw_s,
    gw_r,
    gx_s,
    gx_r,
    gc_s,
    gc_r,
    pm_s,
    pm_r,
    pw_s,
    pw_r,
):
    count = field.shape[-1]
    chips = modes // 2
    rows = count // modes
    piece = rows // waves
    width = count // CUTS
    mode = lax.axis_index("mode")
    wave = lax.axis_index("wave")
    core = lax.rem(mode, 2)
    chip = lax.div(mode, 2)
    other = 1 - core

    loads = [
        pltpu.make_async_copy(src.at[p], dst.at[p], load_s.at[2 * i + p])
        for i, (src, dst) in enumerate(((target_hbm, target), (old_hbm, old), (field_hbm, field)))
        for p in range(2)
    ]
    for copy in loads:
        copy.start()

    barrier = pltpu.get_barrier_semaphore()
    for step in range(1, modes):
        pl.semaphore_signal(
            barrier, inc=1, device_id={"mode": lax.rem(mode + step, modes)}, device_id_type=MESH
        )
    for step in range(1, waves):
        pl.semaphore_signal(
            barrier, inc=1, device_id={"wave": lax.rem(wave + step, waves)}, device_id_type=MESH
        )

    def partner(me, size, step):
        if size == 4:
            high, low = ((1, 1), (1, 0), (0, 1))[step - 1]
            to = 2 * lax.rem(lax.div(me, 2) + high, 2) + lax.rem(lax.rem(me, 2) + low, 2)
            return to, to
        return lax.rem(me + step, size), lax.rem(me - step + size, size)

    chip_to = [partner(chip, chips, step) for step in range(1, chips)]
    wave_to = [partner(wave, waves, step) for step in range(1, waves)]
    pending = []

    def send(src, dst, s_sem, r_sem, to):
        copy = pltpu.make_async_remote_copy(
            src_ref=src, dst_ref=dst, send_sem=s_sem, recv_sem=r_sem, device_id=to, device_id_type=MESH
        )
        copy.start()
        pending.append(copy)
        return copy

    def starts_of(which):
        return [pl.multiple_of((2 * q + which) * rows, rows) for q in range(chips)]

    def right_rows(low, starts, cut):
        size = rows * len(starts)
        for half, base in ((0, count), (1, 0)):
            result = jnp.dot(
                joined[pl.ds(low, size), :],
                right[:, pl.ds(half * count + cut * width, width)],
                preferred_element_type=F32,
            ).astype(BF16)
            for q, start in enumerate(starts):
                middle[pl.ds(pl.multiple_of(base + start, rows), rows), pl.ds(cut * width, width)] = result[
                    q * rows : (q + 1) * rows
                ]

    def left_half(trip, cut, which, term):
        starts = starts_of(which)
        cols = pl.ds(cut * width, width)
        lhs = jnp.concatenate(
            [right[pl.ds(s, rows), :] for s in starts]
            + [right[pl.ds(pl.multiple_of(count + s, rows), rows), :] for s in starts],
            0,
        )
        result = jnp.dot(lhs, middle[:, cols], preferred_element_type=F32)
        for q in range(chips):
            im = result[q * rows : (q + 1) * rows]
            re = result[(chips + q) * rows : (chips + q + 1) * rows]
            term_re, term_im = term(re, im, pl.ds(starts[q], rows), cols)
            part[trip, cut, which, q, :, pl.ds(0, width)] = term_re.astype(BF16)
            part[trip, cut, which, q, :, pl.ds(width, width)] = term_im.astype(BF16)

    def reduce_scatter(trip, prepare, term, ready, arrived):
        crossings = []
        for cut in range(CUTS):
            prepare(cut)
            left_half(trip, cut, other, term)
            if cut == 0:
                ready()
            crossings.append(
                send(
                    part.at[trip, cut, other],
                    core_in.at[trip, cut],
                    core_s.at[trip, cut],
                    core_r.at[trip, cut],
                    {"mode": 2 * chip + other},
                )
            )
        fans = []
        for cut in range(CUTS):
            left_half(trip, cut, core, term)
            crossings[cut].wait_recv()
            fan = []
            for step, (to, _) in enumerate(chip_to, 1):
                chip_out[trip, cut, step] = (
                    part[trip, cut, core, to].astype(F32) + core_in[trip, cut, to].astype(F32)
                ).astype(BF16)
                fan.append(
                    send(
                        chip_out.at[trip, cut, step],
                        chip_in.at[trip, cut, step],
                        chip_s.at[trip, cut, step],
                        chip_r.at[trip, cut, step],
                        {"mode": 2 * to + core},
                    )
                )
            fans.append(fan)
        hops = []
        for cut in range(CUTS):
            total = part[trip, cut, core, chip].astype(F32) + core_in[trip, cut, chip].astype(F32)
            for step, copy in enumerate(fans[cut], 1):
                copy.wait_recv()
                total = total + chip_in[trip, cut, step].astype(F32)
            wave_out[trip, cut] = total.astype(BF16).reshape(waves, piece, 2 * width)
            hop = []
            for step, (to, _) in enumerate(wave_to, 1):
                hop.append(
                    send(
                        wave_out.at[trip, cut, to],
                        wave_in.at[trip, cut, step],
                        wave_s.at[trip, cut, step],
                        wave_r.at[trip, cut, step],
                        {"wave": to},
                    )
                )
            hops.append(hop)
        for cut in range(CUTS):
            result = wave_out[trip, cut, wave].astype(F32)
            for step, copy in enumerate(hops[cut], 1):
                copy.wait_recv()
                result = result + wave_in[trip, cut, step].astype(F32)
            arrived(cut, result)

    def folded(values):
        squares = jnp.sum((values * values).reshape(piece // 8, 8, 2 * width), 0)
        tile = squares[:, :LANES]
        for low in range(LANES, 2 * width, LANES):
            tile = tile + squares[:, low : low + LANES]
        return tile

    def power_over_modes(trip, tile):
        power_out[trip] = tile
        return [
            send(
                power_out.at[trip],
                power_in.at[trip, step],
                pm_s.at[trip, step],
                pm_r.at[trip, step],
                {"mode": lax.rem(mode + step, modes)},
            )
            for step in range(1, modes)
        ]

    def power_over_waves(trip, tile, copies):
        for step, copy in enumerate(copies, 1):
            copy.wait_recv()
            tile = tile + power_in[trip, step]
        power_out2[trip] = tile
        return tile, [
            send(
                power_out2.at[trip],
                power_in2.at[trip, step],
                pw_s.at[trip, step],
                pw_r.at[trip, step],
                {"wave": lax.rem(wave + step, waves)},
            )
            for step in range(1, waves)
        ]

    def mean_power(trip, tile, copies):
        for step, copy in enumerate(copies, 1):
            copy.wait_recv()
            tile = tile + power_in2[trip, step]
        return jnp.sum(tile, keepdims=True) / (count * count)

    def phasor(block, power):
        re = block[:, :width].astype(F32)
        im = block[:, width:].astype(F32)
        factor = lax.rsqrt(re * re + im * im + power + 1e-06)
        return (re * factor).astype(BF16), (im * factor).astype(BF16)

    build_right(scale_ref[0], right, count)

    for copy in loads[:4]:
        copy.wait()
    t_re = target[0].astype(F32)
    t_im = target[1].astype(F32)
    o_re = old[0].astype(F32)
    o_im = old[1].astype(F32)
    joined[:, pl.ds(0, count)] = (t_re * o_re + t_im * o_im).astype(BF16)
    joined[:, pl.ds(count, count)] = (t_re * o_im - t_im * o_re).astype(BF16)
    every = [q * rows for q in range(modes)]

    def term_one(re, im, at, cols):
        f_re = field[0, at, cols].astype(F32)
        f_im = field[1, at, cols].astype(F32)
        return re * f_re - im * f_im, -(re * f_im + im * f_re)

    def backward_right(cut):
        right_rows(0, every, cut)
        if cut == 0:
            for copy in loads[4:]:
                copy.wait()

    def entered():
        pl.semaphore_wait(barrier, modes - 1 + waves - 1)

    mine = pl.ds(pl.multiple_of(wave * piece, piece), piece)
    squares = []
    hops = []

    def spread(trip, cut, own, value):
        own[...] = value.astype(BF16)
        hops.append(
            [
                send(
                    own,
                    own,
                    gw_s.at[trip, cut, step],
                    gw_r.at[trip, cut, step],
                    {"wave": to},
                )
                for step, (to, _) in enumerate(wave_to, 1)
            ]
        )
        squares.append(folded(value))

    reduce_scatter(
        0,
        backward_right,
        term_one,
        entered,
        lambda cut, v: spread(0, cut, whole.at[cut, core, chip, mine], v),
    )
    tile = sum(squares[1:], squares[0])
    tiles = power_over_modes(0, tile)
    fans = []
    across = []
    order = []
    for cut in range(CUTS):
        for copy in hops[cut]:
            copy.wait_recv()
        block = whole.at[cut, core, chip]
        fans.append(
            [
                send(
                    block,
                    block,
                    gx_s.at[cut, step],
                    gx_r.at[cut, step],
                    {"mode": 2 * to + core},
                )
                for step, (to, _) in enumerate(chip_to, 1)
            ]
        )
        across.append(send(block, block, gc_s.at[cut, 0], gc_r.at[cut, 0], {"mode": 2 * chip + other}))
        order.append((cut, 0))
    tile, tiles2 = power_over_waves(0, tile, tiles)
    sources = [chip] + [source for _, source in chip_to]
    for cut in range(CUTS):
        for step, copy in enumerate(fans[cut], 1):
            copy.wait_recv()
            came = whole.at[cut, core, sources[step]]
            across.append(
                send(came, came, gc_s.at[cut, step], gc_r.at[cut, step], {"mode": 2 * chip + other})
            )
            order.append((cut, step))
    power = mean_power(0, tile, tiles2)

    def masked(cut, which, source, at):
        start = pl.multiple_of((2 * source + which) * rows, rows)
        cols = pl.ds(cut * width, width)
        m_re, m_im = phasor(whole[cut, which, source], power)
        n_re = m_re.astype(F32)
        n_im = m_im.astype(F32)
        f_re = field[0, pl.ds(start, rows), cols].astype(F32)
        f_im = field[1, pl.ds(start, rows), cols].astype(F32)
        joined[at, cols] = (f_re * n_re - f_im * n_im).astype(BF16)
        joined[at, pl.ds(count + cut * width, width)] = (f_re * n_im + f_im * n_re).astype(BF16)

    def places(which):
        return [pl.multiple_of((2 * source + which) * rows, rows) for source in sources]

    for step, source in enumerate(sources):
        for cut in range(CUTS):
            masked(cut, core, source, pl.ds(step * rows, rows))
    for cut in range(CUTS):
        right_rows(0, places(core), cut)
    for copy, (cut, step) in zip(across, order):
        copy.wait_recv()
        masked(cut, other, sources[step], pl.ds(count // 2 + step * rows, rows))

    def forward_right(cut):
        right_rows(count // 2, places(other), cut)

    def term_two(re, im, at, cols):
        b_re = target[0, at, cols].astype(F32)
        b_im = target[1, at, cols].astype(F32)
        return b_re * re + b_im * im, b_im * re - b_re * im

    squares.clear()
    hops.clear()
    reduce_scatter(
        1,
        forward_right,
        term_two,
        lambda: None,
        lambda cut, v: spread(1, cut, last.at[cut, mine], v),
    )
    tile = sum(squares[1:], squares[0])
    tiles = power_over_modes(1, tile)
    for cut in range(CUTS):
        cols = pl.ds(cut * width, width)
        m_re, m_im = phasor(whole[cut, core, chip], power)
        masks[0, :, cols] = m_re
        masks[1, :, cols] = m_im
    tile, tiles2 = power_over_waves(1, tile, tiles)
    for hop in hops:
        for copy in hop:
            copy.wait_recv()
    power = mean_power(1, tile, tiles2)
    for cut in range(CUTS):
        cols = pl.ds(cut * width, width)
        m_re, m_im = phasor(last[cut], power)
        masks[2, :, cols] = m_re
        masks[3, :, cols] = m_im
    for copy in pending:
        copy.wait_send()


def fused(field_in, target, mask_old, scales):
    modes = lax.axis_size("mode")
    waves = lax.axis_size("wave")
    count = field_in.shape[-1]
    chips = modes // 2
    rows = count // modes
    piece = rows // waves
    wide = 2 * count // CUTS
    dma = pltpu.SemaphoreType.DMA
    out = jax.ShapeDtypeStruct((4, rows, count), BF16)
    vmem = pl.BlockSpec(memory_space=pltpu.VMEM)
    anywhere = pl.BlockSpec(memory_space=pl.ANY)
    masks = pl.pallas_call(
        functools.partial(kernel, modes, waves),
        out_shape=out,
        in_specs=[pl.BlockSpec(memory_space=pltpu.SMEM), anywhere, anywhere, anywhere],
        out_specs=vmem,
        scratch_shapes=[
            pltpu.VMEM((2, count, count), BF16),
            pltpu.VMEM((2, count, count), BF16),
            pltpu.VMEM((2, count, count), BF16),
            pltpu.VMEM((2 * count, 2 * count), BF16),
            pltpu.VMEM((count, 2 * count), BF16),
            pltpu.VMEM((2 * count, count), BF16),
            pltpu.VMEM((2, CUTS, 2, chips, rows, wide), BF16),
            pltpu.VMEM((2, CUTS, chips, rows, wide), BF16),
            pltpu.VMEM((2, CUTS, chips, rows, wide), BF16),
            pltpu.VMEM((2, CUTS, chips, rows, wide), BF16),
            pltpu.VMEM((2, CUTS, waves, piece, wide), BF16),
            pltpu.VMEM((2, CUTS, waves, piece, wide), BF16),
            pltpu.VMEM((CUTS, 2, chips, rows, wide), BF16),
            pltpu.VMEM((CUTS, rows, wide), BF16),
            pltpu.VMEM((2, 8, LANES), F32),
            pltpu.VMEM((2, modes, 8, LANES), F32),
            pltpu.VMEM((2, 8, LANES), F32),
            pltpu.VMEM((2, waves, 8, LANES), F32),
            dma((6,)),
            dma((2, CUTS)),
            dma((2, CUTS)),
            dma((2, CUTS, chips)),
            dma((2, CUTS, chips)),
            dma((2, CUTS, waves)),
            dma((2, CUTS, waves)),
            dma((2, CUTS, waves)),
            dma((2, CUTS, waves)),
            dma((CUTS, chips)),
            dma((CUTS, chips)),
            dma((CUTS, chips)),
            dma((CUTS, chips)),
            dma((2, modes)),
            dma((2, modes)),
            dma((2, waves)),
            dma((2, waves)),
        ],
        compiler_params=pltpu.CompilerParams(
            collective_id=0, has_side_effects=True, vmem_limit_bytes=56 * 1024 * 1024
        ),
        cost_estimate=pl.CostEstimate(flops=16 * count**3 * 2, bytes_accessed=12 * count**2, transcendentals=0),
    )(scales, field_in[0, 0], target[0, 0], mask_old)
    return masks[:2], masks[2:]


def chirp(scale, count):
    pos = jnp.arange(count, dtype=jnp.float32)
    diff = pos[:, None] - pos[None, :]
    angle = jnp.pi * scale * diff * diff / count
    factor = jnp.float32(count) ** (-0.5)
    return (
        (jnp.cos(angle) * factor).astype(jnp.bfloat16),
        (jnp.sin(angle) * factor).astype(jnp.bfloat16),
    )


def right_matrix(real_part, imag_part, sign):
    upper = jnp.concatenate([real_part, sign * imag_part], 1)
    lower = jnp.concatenate([-sign * imag_part, real_part], 1)
    return jnp.concatenate([upper, lower], 0)


def left_matrix(real_part, imag_part, sign):
    first = jnp.concatenate([real_part, sign * imag_part], 0)
    second = jnp.concatenate([-sign * imag_part, real_part], 0)
    return jnp.stack([first, second], 0)


def right_product(field_re, field_im, right):
    joined = jnp.concatenate([field_re, field_im], -1)
    return jnp.einsum("brk,kc->brc", joined, right, preferred_element_type=jnp.float32).astype(
        jnp.bfloat16
    )


def left_product(middle, left):
    batch = middle.shape[0]
    count = middle.shape[1]
    shaped = middle.reshape(batch, count, 2, count)
    result = jnp.einsum("pqk,bkpc->bqc", left, shaped, preferred_element_type=jnp.float32)
    return (result[:, :count], result[:, count:])


def phasor_rows(total, power_sum, count):
    power = power_sum / (count * count)
    real_part = total[:, :count]
    imag_part = total[:, count:]
    factor = lax.rsqrt(real_part * real_part + imag_part * imag_part + power + 1e-06)
    return jnp.concatenate([real_part * factor, imag_part * factor], -1).astype(jnp.bfloat16)


def as_output(mask_part, count):
    return jnp.stack([mask_part[:, :count], mask_part[:, count:]], 0)


def whole_mask(term):
    total = lax.psum(term, ("mode", "wave"))
    return phasor_rows(total, jnp.sum(total * total), term.shape[1] // 2)


def local(field_in, target, mask_old, scales):
    count = field_in.shape[-1]
    row_count = count // lax.axis_size("mode")
    kernel_re, kernel_im = chirp(scales[0], count)
    f_re = field_in[0, :, 0]
    f_im = field_in[0, :, 1]
    b_re = target[0, :, 0].astype(jnp.float32)
    b_im = target[0, :, 1].astype(jnp.float32)
    old_re = mask_old[0].astype(jnp.float32)
    old_im = mask_old[1].astype(jnp.float32)
    c_re = (b_re * old_re + b_im * old_im).astype(jnp.bfloat16)
    c_im = (b_im * old_re - b_re * old_im).astype(jnp.bfloat16)
    middle = right_product(c_re, c_im, right_matrix(kernel_re, kernel_im, -1.0))
    back_re, back_im = left_product(middle, left_matrix(kernel_re, kernel_im, -1.0))
    fr32 = f_re.astype(jnp.float32)
    fi32 = f_im.astype(jnp.float32)
    term_one = jnp.concatenate(
        [jnp.sum(back_re * fr32 + back_im * fi32, 0), jnp.sum(back_im * fr32 - back_re * fi32, 0)],
        -1,
    )
    forward_right = right_matrix(kernel_re, kernel_im, 1.0)
    mask_full = whole_mask(term_one)
    new_re = mask_full[:, :count].astype(jnp.float32)
    new_im = mask_full[:, count:].astype(jnp.float32)
    g_re = (fr32 * new_re - fi32 * new_im).astype(jnp.bfloat16)
    g_im = (fr32 * new_im + fi32 * new_re).astype(jnp.bfloat16)
    ahead_mid = right_product(g_re, g_im, forward_right)
    first_rows = lax.dynamic_slice_in_dim(
        mask_full, lax.axis_index("mode") * row_count, row_count, 0
    )
    ahead_re, ahead_im = left_product(ahead_mid, left_matrix(kernel_re, kernel_im, 1.0))
    term_two = jnp.concatenate(
        [
            jnp.sum(b_re * ahead_re + b_im * ahead_im, 0),
            jnp.sum(b_im * ahead_re - b_re * ahead_im, 0),
        ],
        -1,
    )
    second_full = whole_mask(term_two)
    second_rows = lax.dynamic_slice_in_dim(
        second_full, lax.axis_index("mode") * row_count, row_count, 0
    )
    return (as_output(first_rows, count), as_output(second_rows, count))


def solution(mesh):
    in_specs = (
        P("wave", "mode", None, None, None),
        P("wave", "mode", None, None, None),
        P(),
        P("wave"),
    )
    out_specs = (P(None, "mode", None), P(None, "mode", None))
    modes, waves = mesh.shape["mode"], mesh.shape["wave"]

    def step(field_in, target, mask_old, scales):
        count = field_in.shape[-1]
        single = field_in.shape[0] == waves and field_in.shape[1] == modes
        fits = modes % 2 == 0 and count % (modes * waves * SUB) == 0 and count % (CUTS * LANES) == 0
        body = fused if single and fits else local
        return jax.shard_map(body, mesh=mesh, in_specs=in_specs, out_specs=out_specs, check_vma=False)(
            field_in, target, mask_old, scales
        )

    return step
```

```python
import functools

import jax
import jax.numpy as jnp
from jax import lax
from jax.experimental import pallas as pl
from jax.experimental.pallas import tpu as pltpu
from jax.sharding import PartitionSpec as P

MESH = pl.DeviceIdType.MESH
F32 = jnp.float32
BF16 = jnp.bfloat16
SUB = 16
LANES = 128
CUTS = 2


def build_right(scale, right, count):
    wide = 2 * count
    half = SUB // 2
    row = lax.broadcasted_iota(jnp.int32, (half, wide), 0)
    col = lax.broadcasted_iota(jnp.int32, (half, wide), 1)
    diff = (row - col + count).astype(F32)
    angle = (jnp.pi * scale) * diff * diff / count
    factor = float(count) ** (-0.5)
    top_re = jnp.cos(angle) * factor
    top_im = jnp.sin(angle) * factor
    base_re = jnp.concatenate([top_re, pltpu.roll(top_re, half, 1)], 0)
    base_im = jnp.concatenate([top_im, pltpu.roll(top_im, half, 1)], 0)
    for shift in range(0, LANES, SUB):
        re = (pltpu.roll(base_re, shift, 1) if shift else base_re).astype(BF16)
        im = (pltpu.roll(base_im, shift, 1) if shift else base_im).astype(BF16)
        for hop in range(count // LANES):
            top = hop * LANES + shift
            begin = count - hop * LANES
            k_re = re[:, begin : begin + count]
            k_im = im[:, begin : begin + count]
            right[pl.ds(top, SUB), pl.ds(0, count)] = k_re
            right[pl.ds(top, SUB), pl.ds(count, count)] = k_im
            right[pl.ds(count + top, SUB), pl.ds(0, count)] = -k_im
            right[pl.ds(count + top, SUB), pl.ds(count, count)] = k_re


def kernel(
    modes,
    waves,
    scale_ref,
    field_hbm,
    target_hbm,
    old_hbm,
    masks,
    field,
    target,
    old,
    right,
    joined,
    middle,
    part,
    core_in,
    chip_out,
    chip_in,
    wave_out,
    wave_in,
    whole,
    last,
    power_out,
    power_in,
    power_out2,
    power_in2,
    load_s,
    core_s,
    core_r,
    chip_s,
    chip_r,
    wave_s,
    wave_r,
    gw_s,
    gw_r,
    gx_s,
    gx_r,
    gc_s,
    gc_r,
    pm_s,
    pm_r,
    pw_s,
    pw_r,
):
    count = field.shape[-1]
    chips = modes // 2
    rows = count // modes
    piece = rows // waves
    width = count // CUTS
    mode = lax.axis_index("mode")
    wave = lax.axis_index("wave")
    core = lax.rem(mode, 2)
    chip = lax.div(mode, 2)
    other = 1 - core

    loads = [
        pltpu.make_async_copy(src.at[p], dst.at[p], load_s.at[2 * i + p])
        for i, (src, dst) in enumerate(((target_hbm, target), (old_hbm, old), (field_hbm, field)))
        for p in range(2)
    ]
    for copy in loads:
        copy.start()

    barrier = pltpu.get_barrier_semaphore()
    for step in range(1, modes):
        pl.semaphore_signal(
            barrier, inc=1, device_id={"mode": lax.rem(mode + step, modes)}, device_id_type=MESH
        )
    for step in range(1, waves):
        pl.semaphore_signal(
            barrier, inc=1, device_id={"wave": lax.rem(wave + step, waves)}, device_id_type=MESH
        )

    def partner(me, size, step, turns):
        if size == 4:
            high, low = turns[step - 1]
            to = 2 * lax.rem(lax.div(me, 2) + high, 2) + lax.rem(lax.rem(me, 2) + low, 2)
            return to, to
        return lax.rem(me + step, size), lax.rem(me - step + size, size)

    chip_to = [partner(chip, chips, step, ((core, other), (other, core), (1, 1))) for step in range(1, chips)]
    other_to = [partner(chip, chips, step, ((other, core), (core, other), (1, 1))) for step in range(1, chips)]
    wave_to = [partner(wave, waves, step, ((1, 0), (1, 1), (0, 1))) for step in range(1, waves)]
    pending = []

    def send(src, dst, s_sem, r_sem, to):
        copy = pltpu.make_async_remote_copy(
            src_ref=src, dst_ref=dst, send_sem=s_sem, recv_sem=r_sem, device_id=to, device_id_type=MESH
        )
        copy.start()
        pending.append(copy)
        return copy

    def starts_of(which):
        return [pl.multiple_of((2 * q + which) * rows, rows) for q in range(chips)]

    def right_rows(low, starts, cut):
        size = rows * len(starts)
        for half, base in ((0, count), (1, 0)):
            result = jnp.dot(
                joined[pl.ds(low, size), :],
                right[:, pl.ds(half * count + cut * width, width)],
                preferred_element_type=F32,
            ).astype(BF16)
            for q, start in enumerate(starts):
                middle[pl.ds(pl.multiple_of(base + start, rows), rows), pl.ds(cut * width, width)] = result[
                    q * rows : (q + 1) * rows
                ]

    def left_half(trip, cut, which, term):
        starts = starts_of(which)
        cols = pl.ds(cut * width, width)
        lhs = jnp.concatenate(
            [right[pl.ds(s, rows), :] for s in starts]
            + [right[pl.ds(pl.multiple_of(count + s, rows), rows), :] for s in starts],
            0,
        )
        result = jnp.dot(lhs, middle[:, cols], preferred_element_type=F32)
        for q in range(chips):
            im = result[q * rows : (q + 1) * rows]
            re = result[(chips + q) * rows : (chips + q + 1) * rows]
            term_re, term_im = term(re, im, pl.ds(starts[q], rows), cols)
            part[trip, cut, which, q, :, pl.ds(0, width)] = term_re.astype(BF16)
            part[trip, cut, which, q, :, pl.ds(width, width)] = term_im.astype(BF16)

    def reduce_scatter(trip, prepare, term, ready, arrived):
        crossings = []
        for cut in range(CUTS):
            prepare(cut)
            left_half(trip, cut, other, term)
            if cut == 0:
                ready()
            crossings.append(
                send(
                    part.at[trip, cut, other],
                    core_in.at[trip, cut],
                    core_s.at[trip, cut],
                    core_r.at[trip, cut],
                    {"mode": 2 * chip + other},
                )
            )
        fans = []
        for cut in range(CUTS):
            left_half(trip, cut, core, term)
            crossings[cut].wait_recv()
            fan = []
            for step, (to, _) in enumerate(chip_to, 1):
                chip_out[trip, cut, step] = (
                    part[trip, cut, core, to].astype(F32) + core_in[trip, cut, to].astype(F32)
                ).astype(BF16)
                fan.append(
                    send(
                        chip_out.at[trip, cut, step],
                        chip_in.at[trip, cut, step],
                        chip_s.at[trip, cut, step],
                        chip_r.at[trip, cut, step],
                        {"mode": 2 * to + core},
                    )
                )
            fans.append(fan)
        hops = []
        for cut in range(CUTS):
            total = part[trip, cut, core, chip].astype(F32) + core_in[trip, cut, chip].astype(F32)
            for step, copy in enumerate(fans[cut], 1):
                copy.wait_recv()
                total = total + chip_in[trip, cut, step].astype(F32)
            wave_out[trip, cut] = total.astype(BF16).reshape(waves, piece, 2 * width)
            hop = []
            for step, (to, _) in enumerate(wave_to, 1):
                hop.append(
                    send(
                        wave_out.at[trip, cut, to],
                        wave_in.at[trip, cut, step],
                        wave_s.at[trip, cut, step],
                        wave_r.at[trip, cut, step],
                        {"wave": to},
                    )
                )
            hops.append(hop)
        for cut in range(CUTS):
            result = wave_out[trip, cut, wave].astype(F32)
            for step, copy in enumerate(hops[cut], 1):
                copy.wait_recv()
                result = result + wave_in[trip, cut, step].astype(F32)
            arrived(cut, result)

    def folded(values):
        squares = jnp.sum((values * values).reshape(piece // 8, 8, 2 * width), 0)
        tile = squares[:, :LANES]
        for low in range(LANES, 2 * width, LANES):
            tile = tile + squares[:, low : low + LANES]
        return tile

    def power_over_modes(trip, tile):
        power_out[trip] = tile
        return [
            send(
                power_out.at[trip],
                power_in.at[trip, step],
                pm_s.at[trip, step],
                pm_r.at[trip, step],
                {"mode": lax.rem(mode + step, modes)},
            )
            for step in range(1, modes)
        ]

    def power_over_waves(trip, tile, copies):
        for step, copy in enumerate(copies, 1):
            copy.wait_recv()
            tile = tile + power_in[trip, step]
        power_out2[trip] = tile
        return tile, [
            send(
                power_out2.at[trip],
                power_in2.at[trip, step],
                pw_s.at[trip, step],
                pw_r.at[trip, step],
                {"wave": lax.rem(wave + step, waves)},
            )
            for step in range(1, waves)
        ]

    def mean_power(trip, tile, copies):
        for step, copy in enumerate(copies, 1):
            copy.wait_recv()
            tile = tile + power_in2[trip, step]
        return jnp.sum(tile, keepdims=True) / (count * count)

    def phasor(block, power):
        re = block[:, :width].astype(F32)
        im = block[:, width:].astype(F32)
        factor = lax.rsqrt(re * re + im * im + power + 1e-06)
        return (re * factor).astype(BF16), (im * factor).astype(BF16)

    build_right(scale_ref[0], right, count)

    for copy in loads[:4]:
        copy.wait()
    t_re = target[0].astype(F32)
    t_im = target[1].astype(F32)
    o_re = old[0].astype(F32)
    o_im = old[1].astype(F32)
    joined[:, pl.ds(0, count)] = (t_re * o_re + t_im * o_im).astype(BF16)
    joined[:, pl.ds(count, count)] = (t_re * o_im - t_im * o_re).astype(BF16)
    every = [q * rows for q in range(modes)]

    def term_one(re, im, at, cols):
        f_re = field[0, at, cols].astype(F32)
        f_im = field[1, at, cols].astype(F32)
        return re * f_re - im * f_im, -(re * f_im + im * f_re)

    def backward_right(cut):
        right_rows(0, every, cut)
        if cut == 0:
            for copy in loads[4:]:
                copy.wait()

    def entered():
        pl.semaphore_wait(barrier, modes - 1 + waves - 1)

    mine = pl.ds(pl.multiple_of(wave * piece, piece), piece)
    squares = []
    hops = []

    def spread(trip, cut, own, value):
        own[...] = value.astype(BF16)
        hops.append(
            [
                send(
                    own,
                    own,
                    gw_s.at[trip, cut, step],
                    gw_r.at[trip, cut, step],
                    {"wave": to},
                )
                for step, (to, _) in enumerate(wave_to, 1)
            ]
        )
        squares.append(folded(value))

    reduce_scatter(
        0,
        backward_right,
        term_one,
        entered,
        lambda cut, v: spread(0, cut, whole.at[cut, core, chip, mine], v),
    )
    tile = sum(squares[1:], squares[0])
    tiles = power_over_modes(0, tile)
    fans = []
    across = []
    order = []
    for cut in range(CUTS):
        for copy in hops[cut]:
            copy.wait_recv()
        block = whole.at[cut, core, chip]
        fans.append(
            [
                send(
                    block,
                    block,
                    gx_s.at[cut, step],
                    gx_r.at[cut, step],
                    {"mode": 2 * to + core},
                )
                for step, (to, _) in enumerate(chip_to, 1)
            ]
        )
        across.append(send(block, block, gc_s.at[cut, 0], gc_r.at[cut, 0], {"mode": 2 * chip + other}))
        order.append((cut, 0))
    tile, tiles2 = power_over_waves(0, tile, tiles)
    sources = [chip] + [source for _, source in chip_to]
    others = [chip] + [source for _, source in other_to]
    for cut in range(CUTS):
        for step, copy in enumerate(fans[cut], 1):
            copy.wait_recv()
            came = whole.at[cut, core, sources[step]]
            across.append(
                send(came, came, gc_s.at[cut, step], gc_r.at[cut, step], {"mode": 2 * chip + other})
            )
            order.append((cut, step))
    power = mean_power(0, tile, tiles2)

    def masked(cut, which, source, at):
        start = pl.multiple_of((2 * source + which) * rows, rows)
        cols = pl.ds(cut * width, width)
        m_re, m_im = phasor(whole[cut, which, source], power)
        n_re = m_re.astype(F32)
        n_im = m_im.astype(F32)
        f_re = field[0, pl.ds(start, rows), cols].astype(F32)
        f_im = field[1, pl.ds(start, rows), cols].astype(F32)
        joined[at, cols] = (f_re * n_re - f_im * n_im).astype(BF16)
        joined[at, pl.ds(count + cut * width, width)] = (f_re * n_im + f_im * n_re).astype(BF16)

    def places(which, chain):
        return [pl.multiple_of((2 * source + which) * rows, rows) for source in chain]

    for step, source in enumerate(sources):
        for cut in range(CUTS):
            masked(cut, core, source, pl.ds(step * rows, rows))
    for cut in range(CUTS):
        right_rows(0, places(core, sources), cut)
    for copy, (cut, step) in zip(across, order):
        copy.wait_recv()
        masked(cut, other, others[step], pl.ds(count // 2 + step * rows, rows))

    def forward_right(cut):
        right_rows(count // 2, places(other, others), cut)

    def term_two(re, im, at, cols):
        b_re = target[0, at, cols].astype(F32)
        b_im = target[1, at, cols].astype(F32)
        return b_re * re + b_im * im, b_im * re - b_re * im

    squares.clear()
    hops.clear()
    reduce_scatter(
        1,
        forward_right,
        term_two,
        lambda: None,
        lambda cut, v: spread(1, cut, last.at[cut, mine], v),
    )
    tile = sum(squares[1:], squares[0])
    tiles = power_over_modes(1, tile)
    for cut in range(CUTS):
        cols = pl.ds(cut * width, width)
        m_re, m_im = phasor(whole[cut, core, chip], power)
        masks[0, :, cols] = m_re
        masks[1, :, cols] = m_im
    tile, tiles2 = power_over_waves(1, tile, tiles)
    for hop in hops:
        for copy in hop:
            copy.wait_recv()
    power = mean_power(1, tile, tiles2)
    for cut in range(CUTS):
        cols = pl.ds(cut * width, width)
        m_re, m_im = phasor(last[cut], power)
        masks[2, :, cols] = m_re
        masks[3, :, cols] = m_im
    for copy in pending:
        copy.wait_send()


def fused(field_in, target, mask_old, scales):
    modes = lax.axis_size("mode")
    waves = lax.axis_size("wave")
    count = field_in.shape[-1]
    chips = modes // 2
    rows = count // modes
    piece = rows // waves
    wide = 2 * count // CUTS
    dma = pltpu.SemaphoreType.DMA
    out = jax.ShapeDtypeStruct((4, rows, count), BF16)
    vmem = pl.BlockSpec(memory_space=pltpu.VMEM)
    anywhere = pl.BlockSpec(memory_space=pl.ANY)
    masks = pl.pallas_call(
        functools.partial(kernel, modes, waves),
        out_shape=out,
        in_specs=[pl.BlockSpec(memory_space=pltpu.SMEM), anywhere, anywhere, anywhere],
        out_specs=vmem,
        scratch_shapes=[
            pltpu.VMEM((2, count, count), BF16),
            pltpu.VMEM((2, count, count), BF16),
            pltpu.VMEM((2, count, count), BF16),
            pltpu.VMEM((2 * count, 2 * count), BF16),
            pltpu.VMEM((count, 2 * count), BF16),
            pltpu.VMEM((2 * count, count), BF16),
            pltpu.VMEM((2, CUTS, 2, chips, rows, wide), BF16),
            pltpu.VMEM((2, CUTS, chips, rows, wide), BF16),
            pltpu.VMEM((2, CUTS, chips, rows, wide), BF16),
            pltpu.VMEM((2, CUTS, chips, rows, wide), BF16),
            pltpu.VMEM((2, CUTS, waves, piece, wide), BF16),
            pltpu.VMEM((2, CUTS, waves, piece, wide), BF16),
            pltpu.VMEM((CUTS, 2, chips, rows, wide), BF16),
            pltpu.VMEM((CUTS, rows, wide), BF16),
            pltpu.VMEM((2, 8, LANES), F32),
            pltpu.VMEM((2, modes, 8, LANES), F32),
            pltpu.VMEM((2, 8, LANES), F32),
            pltpu.VMEM((2, waves, 8, LANES), F32),
            dma((6,)),
            dma((2, CUTS)),
            dma((2, CUTS)),
            dma((2, CUTS, chips)),
            dma((2, CUTS, chips)),
            dma((2, CUTS, waves)),
            dma((2, CUTS, waves)),
            dma((2, CUTS, waves)),
            dma((2, CUTS, waves)),
            dma((CUTS, chips)),
            dma((CUTS, chips)),
            dma((CUTS, chips)),
            dma((CUTS, chips)),
            dma((2, modes)),
            dma((2, modes)),
            dma((2, waves)),
            dma((2, waves)),
        ],
        compiler_params=pltpu.CompilerParams(
            collective_id=0, has_side_effects=True, vmem_limit_bytes=56 * 1024 * 1024
        ),
        cost_estimate=pl.CostEstimate(flops=16 * count**3 * 2, bytes_accessed=12 * count**2, transcendentals=0),
    )(scales, field_in[0, 0], target[0, 0], mask_old)
    return masks[:2], masks[2:]


def chirp(scale, count):
    pos = jnp.arange(count, dtype=jnp.float32)
    diff = pos[:, None] - pos[None, :]
    angle = jnp.pi * scale * diff * diff / count
    factor = jnp.float32(count) ** (-0.5)
    return (
        (jnp.cos(angle) * factor).astype(jnp.bfloat16),
        (jnp.sin(angle) * factor).astype(jnp.bfloat16),
    )


def right_matrix(real_part, imag_part, sign):
    upper = jnp.concatenate([real_part, sign * imag_part], 1)
    lower = jnp.concatenate([-sign * imag_part, real_part], 1)
    return jnp.concatenate([upper, lower], 0)


def left_matrix(real_part, imag_part, sign):
    first = jnp.concatenate([real_part, sign * imag_part], 0)
    second = jnp.concatenate([-sign * imag_part, real_part], 0)
    return jnp.stack([first, second], 0)


def right_product(field_re, field_im, right):
    joined = jnp.concatenate([field_re, field_im], -1)
    return jnp.einsum("brk,kc->brc", joined, right, preferred_element_type=jnp.float32).astype(
        jnp.bfloat16
    )


def left_product(middle, left):
    batch = middle.shape[0]
    count = middle.shape[1]
    shaped = middle.reshape(batch, count, 2, count)
    result = jnp.einsum("pqk,bkpc->bqc", left, shaped, preferred_element_type=jnp.float32)
    return (result[:, :count], result[:, count:])


def phasor_rows(total, power_sum, count):
    power = power_sum / (count * count)
    real_part = total[:, :count]
    imag_part = total[:, count:]
    factor = lax.rsqrt(real_part * real_part + imag_part * imag_part + power + 1e-06)
    return jnp.concatenate([real_part * factor, imag_part * factor], -1).astype(jnp.bfloat16)


def as_output(mask_part, count):
    return jnp.stack([mask_part[:, :count], mask_part[:, count:]], 0)


def whole_mask(term):
    total = lax.psum(term, ("mode", "wave"))
    return phasor_rows(total, jnp.sum(total * total), term.shape[1] // 2)


def local(field_in, target, mask_old, scales):
    count = field_in.shape[-1]
    row_count = count // lax.axis_size("mode")
    kernel_re, kernel_im = chirp(scales[0], count)
    f_re = field_in[0, :, 0]
    f_im = field_in[0, :, 1]
    b_re = target[0, :, 0].astype(jnp.float32)
    b_im = target[0, :, 1].astype(jnp.float32)
    old_re = mask_old[0].astype(jnp.float32)
    old_im = mask_old[1].astype(jnp.float32)
    c_re = (b_re * old_re + b_im * old_im).astype(jnp.bfloat16)
    c_im = (b_im * old_re - b_re * old_im).astype(jnp.bfloat16)
    middle = right_product(c_re, c_im, right_matrix(kernel_re, kernel_im, -1.0))
    back_re, back_im = left_product(middle, left_matrix(kernel_re, kernel_im, -1.0))
    fr32 = f_re.astype(jnp.float32)
    fi32 = f_im.astype(jnp.float32)
    term_one = jnp.concatenate(
        [jnp.sum(back_re * fr32 + back_im * fi32, 0), jnp.sum(back_im * fr32 - back_re * fi32, 0)],
        -1,
    )
    forward_right = right_matrix(kernel_re, kernel_im, 1.0)
    mask_full = whole_mask(term_one)
    new_re = mask_full[:, :count].astype(jnp.float32)
    new_im = mask_full[:, count:].astype(jnp.float32)
    g_re = (fr32 * new_re - fi32 * new_im).astype(jnp.bfloat16)
    g_im = (fr32 * new_im + fi32 * new_re).astype(jnp.bfloat16)
    ahead_mid = right_product(g_re, g_im, forward_right)
    first_rows = lax.dynamic_slice_in_dim(
        mask_full, lax.axis_index("mode") * row_count, row_count, 0
    )
    ahead_re, ahead_im = left_product(ahead_mid, left_matrix(kernel_re, kernel_im, 1.0))
    term_two = jnp.concatenate(
        [
            jnp.sum(b_re * ahead_re + b_im * ahead_im, 0),
            jnp.sum(b_im * ahead_re - b_re * ahead_im, 0),
        ],
        -1,
    )
    second_full = whole_mask(term_two)
    second_rows = lax.dynamic_slice_in_dim(
        second_full, lax.axis_index("mode") * row_count, row_count, 0
    )
    return (as_output(first_rows, count), as_output(second_rows, count))


def solution(mesh):
    in_specs = (
        P("wave", "mode", None, None, None),
        P("wave", "mode", None, None, None),
        P(),
        P("wave"),
    )
    out_specs = (P(None, "mode", None), P(None, "mode", None))
    modes, waves = mesh.shape["mode"], mesh.shape["wave"]

    def step(field_in, target, mask_old, scales):
        count = field_in.shape[-1]
        single = field_in.shape[0] == waves and field_in.shape[1] == modes
        fits = modes % 2 == 0 and count % (modes * waves * SUB) == 0 and count % (CUTS * LANES) == 0
        body = fused if single and fits else local
        return jax.shard_map(body, mesh=mesh, in_specs=in_specs, out_specs=out_specs, check_vma=False)(
            field_in, target, mask_old, scales
        )

    return step
```

```python
import functools

import jax
import jax.numpy as jnp
from jax import lax
from jax.experimental import pallas as pl
from jax.experimental.pallas import tpu as pltpu
from jax.sharding import PartitionSpec as P

MESH = pl.DeviceIdType.MESH
F32 = jnp.float32
BF16 = jnp.bfloat16
SUB = 16
LANES = 128
CUTS = 2


def build_right(scale, right, count):
    wide = 2 * count
    half = SUB // 2
    row = lax.broadcasted_iota(jnp.int32, (half, wide), 0)
    col = lax.broadcasted_iota(jnp.int32, (half, wide), 1)
    diff = (row - col + count).astype(F32)
    angle = (jnp.pi * scale) * diff * diff / count
    factor = float(count) ** (-0.5)
    top_re = jnp.cos(angle) * factor
    top_im = jnp.sin(angle) * factor
    base_re = jnp.concatenate([top_re, pltpu.roll(top_re, half, 1)], 0)
    base_im = jnp.concatenate([top_im, pltpu.roll(top_im, half, 1)], 0)
    for shift in range(0, LANES, SUB):
        re = (pltpu.roll(base_re, shift, 1) if shift else base_re).astype(BF16)
        im = (pltpu.roll(base_im, shift, 1) if shift else base_im).astype(BF16)
        for hop in range(count // LANES):
            top = hop * LANES + shift
            begin = count - hop * LANES
            k_re = re[:, begin : begin + count]
            k_im = im[:, begin : begin + count]
            right[pl.ds(top, SUB), pl.ds(0, count)] = k_re
            right[pl.ds(top, SUB), pl.ds(count, count)] = k_im
            right[pl.ds(count + top, SUB), pl.ds(0, count)] = -k_im
            right[pl.ds(count + top, SUB), pl.ds(count, count)] = k_re


def kernel(
    modes,
    waves,
    scale_ref,
    field_hbm,
    target_hbm,
    old_hbm,
    masks,
    field,
    target,
    old,
    right,
    joined,
    middle,
    part,
    core_in,
    chip_out,
    chip_in,
    wave_out,
    wave_in,
    whole,
    last,
    power_out,
    power_in,
    power_out2,
    power_in2,
    load_s,
    core_s,
    core_r,
    chip_s,
    chip_r,
    wave_s,
    wave_r,
    gw_s,
    gw_r,
    gx_s,
    gx_r,
    gc_s,
    gc_r,
    pm_s,
    pm_r,
    pw_s,
    pw_r,
):
    count = field.shape[-1]
    chips = modes // 2
    rows = count // modes
    piece = rows // waves
    width = count // CUTS
    mode = lax.axis_index("mode")
    wave = lax.axis_index("wave")
    core = lax.rem(mode, 2)
    chip = lax.div(mode, 2)
    other = 1 - core

    loads = [
        pltpu.make_async_copy(src.at[p], dst.at[p], load_s.at[2 * i + p])
        for i, (src, dst) in enumerate(((target_hbm, target), (old_hbm, old), (field_hbm, field)))
        for p in range(2)
    ]
    for copy in loads:
        copy.start()

    barrier = pltpu.get_barrier_semaphore()
    for step in range(1, modes):
        pl.semaphore_signal(
            barrier, inc=1, device_id={"mode": lax.rem(mode + step, modes)}, device_id_type=MESH
        )
    for step in range(1, waves):
        pl.semaphore_signal(
            barrier, inc=1, device_id={"wave": lax.rem(wave + step, waves)}, device_id_type=MESH
        )

    def partner(me, size, step, turns):
        if size == 4:
            high, low = turns[step - 1]
            to = 2 * lax.rem(lax.div(me, 2) + high, 2) + lax.rem(lax.rem(me, 2) + low, 2)
            return to, to
        return lax.rem(me + step, size), lax.rem(me - step + size, size)

    chip_to = [partner(chip, chips, step, ((core, other), (other, core), (1, 1))) for step in range(1, chips)]
    other_to = [partner(chip, chips, step, ((other, core), (core, other), (1, 1))) for step in range(1, chips)]
    wave_to = [partner(wave, waves, step, ((1, 0), (1, 1), (0, 1))) for step in range(1, waves)]
    pending = []

    def send(src, dst, s_sem, r_sem, to):
        copy = pltpu.make_async_remote_copy(
            src_ref=src, dst_ref=dst, send_sem=s_sem, recv_sem=r_sem, device_id=to, device_id_type=MESH
        )
        copy.start()
        pending.append(copy)
        return copy

    def starts_of(which):
        return [pl.multiple_of((2 * q + which) * rows, rows) for q in range(chips)]

    def right_rows(low, starts, cut):
        size = rows * len(starts)
        for half, base in ((0, count), (1, 0)):
            result = jnp.dot(
                joined[pl.ds(low, size), :],
                right[:, pl.ds(half * count + cut * width, width)],
                preferred_element_type=F32,
            ).astype(BF16)
            for q, start in enumerate(starts):
                middle[pl.ds(pl.multiple_of(base + start, rows), rows), pl.ds(cut * width, width)] = result[
                    q * rows : (q + 1) * rows
                ]

    def left_half(trip, cut, which, term):
        starts = starts_of(which)
        cols = pl.ds(cut * width, width)
        lhs = jnp.concatenate(
            [right[pl.ds(s, rows), :] for s in starts]
            + [right[pl.ds(pl.multiple_of(count + s, rows), rows), :] for s in starts],
            0,
        )
        result = jnp.dot(lhs, middle[:, cols], preferred_element_type=F32)
        for q in range(chips):
            im = result[q * rows : (q + 1) * rows]
            re = result[(chips + q) * rows : (chips + q + 1) * rows]
            term_re, term_im = term(re, im, pl.ds(starts[q], rows), cols)
            part[trip, cut, which, q, :, pl.ds(0, width)] = term_re.astype(BF16)
            part[trip, cut, which, q, :, pl.ds(width, width)] = term_im.astype(BF16)

    def reduce_scatter(trip, prepare, term, ready, arrived):
        crossings = []
        for cut in range(CUTS):
            prepare(cut)
            left_half(trip, cut, other, term)
            if cut == 0:
                ready()
            crossings.append(
                send(
                    part.at[trip, cut, other],
                    core_in.at[trip, cut],
                    core_s.at[trip, cut],
                    core_r.at[trip, cut],
                    {"mode": 2 * chip + other},
                )
            )
        fans = []
        for cut in range(CUTS):
            left_half(trip, cut, core, term)
            crossings[cut].wait_recv()
            fan = []
            for step, (to, _) in enumerate(chip_to, 1):
                chip_out[trip, cut, step] = (
                    part[trip, cut, core, to].astype(F32) + core_in[trip, cut, to].astype(F32)
                ).astype(BF16)
                fan.append(
                    send(
                        chip_out.at[trip, cut, step],
                        chip_in.at[trip, cut, step],
                        chip_s.at[trip, cut, step],
                        chip_r.at[trip, cut, step],
                        {"mode": 2 * to + core},
                    )
                )
            fans.append(fan)
        for cut in range(CUTS):
            total = part[trip, cut, core, chip].astype(F32) + core_in[trip, cut, chip].astype(F32)
            for step, copy in enumerate(fans[cut], 1):
                copy.wait_recv()
                total = total + chip_in[trip, cut, step].astype(F32)
            wave_out[trip, :, cut] = total.astype(BF16).reshape(waves, piece, 2 * width)
        hops = [
            send(
                wave_out.at[trip, to],
                wave_in.at[trip, step],
                wave_s.at[trip, step],
                wave_r.at[trip, step],
                {"wave": to},
            )
            for step, (to, _) in enumerate(wave_to, 1)
        ]
        for copy in hops:
            copy.wait_recv()
        for cut in range(CUTS):
            result = wave_out[trip, wave, cut].astype(F32)
            for step in range(1, waves):
                result = result + wave_in[trip, step, cut].astype(F32)
            arrived(cut, result)

    def folded(values):
        squares = jnp.sum((values * values).reshape(piece // 8, 8, 2 * width), 0)
        tile = squares[:, :LANES]
        for low in range(LANES, 2 * width, LANES):
            tile = tile + squares[:, low : low + LANES]
        return tile

    def power_over_modes(trip, tile):
        power_out[trip] = tile
        return [
            send(
                power_out.at[trip],
                power_in.at[trip, step],
                pm_s.at[trip, step],
                pm_r.at[trip, step],
                {"mode": lax.rem(mode + step, modes)},
            )
            for step in range(1, modes)
        ]

    def power_over_waves(trip, tile, copies):
        for step, copy in enumerate(copies, 1):
            copy.wait_recv()
            tile = tile + power_in[trip, step]
        power_out2[trip] = tile
        return tile, [
            send(
                power_out2.at[trip],
                power_in2.at[trip, step],
                pw_s.at[trip, step],
                pw_r.at[trip, step],
                {"wave": lax.rem(wave + step, waves)},
            )
            for step in range(1, waves)
        ]

    def mean_power(trip, tile, copies):
        for step, copy in enumerate(copies, 1):
            copy.wait_recv()
            tile = tile + power_in2[trip, step]
        return jnp.sum(tile, keepdims=True) / (count * count)

    def phasor(block, power):
        re = block[:, :width].astype(F32)
        im = block[:, width:].astype(F32)
        factor = lax.rsqrt(re * re + im * im + power + 1e-06)
        return (re * factor).astype(BF16), (im * factor).astype(BF16)

    build_right(scale_ref[0], right, count)

    for copy in loads[:4]:
        copy.wait()
    t_re = target[0].astype(F32)
    t_im = target[1].astype(F32)
    o_re = old[0].astype(F32)
    o_im = old[1].astype(F32)
    joined[:, pl.ds(0, count)] = (t_re * o_re + t_im * o_im).astype(BF16)
    joined[:, pl.ds(count, count)] = (t_re * o_im - t_im * o_re).astype(BF16)
    every = [q * rows for q in range(modes)]

    def term_one(re, im, at, cols):
        f_re = field[0, at, cols].astype(F32)
        f_im = field[1, at, cols].astype(F32)
        return re * f_re - im * f_im, -(re * f_im + im * f_re)

    def backward_right(cut):
        right_rows(0, every, cut)
        if cut == 0:
            for copy in loads[4:]:
                copy.wait()

    def entered():
        pl.semaphore_wait(barrier, modes - 1 + waves - 1)

    mine = pl.ds(pl.multiple_of(wave * piece, piece), piece)
    squares = []

    def keep(own, cut, value):
        own[cut] = value.astype(BF16)
        squares.append(folded(value))

    def spread(trip, own):
        return [
            send(own, own, gw_s.at[trip, step], gw_r.at[trip, step], {"wave": to})
            for step, (to, _) in enumerate(wave_to, 1)
        ]

    reduce_scatter(
        0,
        backward_right,
        term_one,
        entered,
        lambda cut, v: keep(whole.at[:, core, chip, mine], cut, v),
    )
    hops = spread(0, whole.at[:, core, chip, mine])
    tile = sum(squares[1:], squares[0])
    tiles = power_over_modes(0, tile)
    for copy in hops:
        copy.wait_recv()
    block = whole.at[:, core, chip]
    fan = [
        send(block, block, gx_s.at[step], gx_r.at[step], {"mode": 2 * to + core})
        for step, (to, _) in enumerate(chip_to, 1)
    ]
    across = [send(block, block, gc_s.at[0], gc_r.at[0], {"mode": 2 * chip + other})]
    tile, tiles2 = power_over_waves(0, tile, tiles)
    sources = [chip] + [source for _, source in chip_to]
    others = [chip] + [source for _, source in other_to]
    for step, copy in enumerate(fan, 1):
        copy.wait_recv()
        came = whole.at[:, core, sources[step]]
        across.append(send(came, came, gc_s.at[step], gc_r.at[step], {"mode": 2 * chip + other}))
    power = mean_power(0, tile, tiles2)

    def masked(cut, which, source, at):
        start = pl.multiple_of((2 * source + which) * rows, rows)
        cols = pl.ds(cut * width, width)
        m_re, m_im = phasor(whole[cut, which, source], power)
        n_re = m_re.astype(F32)
        n_im = m_im.astype(F32)
        f_re = field[0, pl.ds(start, rows), cols].astype(F32)
        f_im = field[1, pl.ds(start, rows), cols].astype(F32)
        joined[at, cols] = (f_re * n_re - f_im * n_im).astype(BF16)
        joined[at, pl.ds(count + cut * width, width)] = (f_re * n_im + f_im * n_re).astype(BF16)

    def places(which, chain):
        return [pl.multiple_of((2 * source + which) * rows, rows) for source in chain]

    for step, source in enumerate(sources):
        for cut in range(CUTS):
            masked(cut, core, source, pl.ds(step * rows, rows))
    for cut in range(CUTS):
        right_rows(0, places(core, sources), cut)
    for step, copy in enumerate(across):
        copy.wait_recv()
        for cut in range(CUTS):
            masked(cut, other, others[step], pl.ds(count // 2 + step * rows, rows))

    def forward_right(cut):
        right_rows(count // 2, places(other, others), cut)

    def term_two(re, im, at, cols):
        b_re = target[0, at, cols].astype(F32)
        b_im = target[1, at, cols].astype(F32)
        return b_re * re + b_im * im, b_im * re - b_re * im

    squares.clear()
    reduce_scatter(
        1,
        forward_right,
        term_two,
        lambda: None,
        lambda cut, v: keep(last.at[:, mine], cut, v),
    )
    tile = sum(squares[1:], squares[0])
    tiles = power_over_modes(1, tile)
    hops = spread(1, last.at[:, mine])
    for cut in range(CUTS):
        cols = pl.ds(cut * width, width)
        m_re, m_im = phasor(whole[cut, core, chip], power)
        masks[0, :, cols] = m_re
        masks[1, :, cols] = m_im
    tile, tiles2 = power_over_waves(1, tile, tiles)
    for copy in hops:
        copy.wait_recv()
    power = mean_power(1, tile, tiles2)
    for cut in range(CUTS):
        cols = pl.ds(cut * width, width)
        m_re, m_im = phasor(last[cut], power)
        masks[2, :, cols] = m_re
        masks[3, :, cols] = m_im
    for copy in pending:
        copy.wait_send()


def fused(field_in, target, mask_old, scales):
    modes = lax.axis_size("mode")
    waves = lax.axis_size("wave")
    count = field_in.shape[-1]
    chips = modes // 2
    rows = count // modes
    piece = rows // waves
    wide = 2 * count // CUTS
    dma = pltpu.SemaphoreType.DMA
    out = jax.ShapeDtypeStruct((4, rows, count), BF16)
    vmem = pl.BlockSpec(memory_space=pltpu.VMEM)
    anywhere = pl.BlockSpec(memory_space=pl.ANY)
    masks = pl.pallas_call(
        functools.partial(kernel, modes, waves),
        out_shape=out,
        in_specs=[pl.BlockSpec(memory_space=pltpu.SMEM), anywhere, anywhere, anywhere],
        out_specs=vmem,
        scratch_shapes=[
            pltpu.VMEM((2, count, count), BF16),
            pltpu.VMEM((2, count, count), BF16),
            pltpu.VMEM((2, count, count), BF16),
            pltpu.VMEM((2 * count, 2 * count), BF16),
            pltpu.VMEM((count, 2 * count), BF16),
            pltpu.VMEM((2 * count, count), BF16),
            pltpu.VMEM((2, CUTS, 2, chips, rows, wide), BF16),
            pltpu.VMEM((2, CUTS, chips, rows, wide), BF16),
            pltpu.VMEM((2, CUTS, chips, rows, wide), BF16),
            pltpu.VMEM((2, CUTS, chips, rows, wide), BF16),
            pltpu.VMEM((2, waves, CUTS, piece, wide), BF16),
            pltpu.VMEM((2, waves, CUTS, piece, wide), BF16),
            pltpu.VMEM((CUTS, 2, chips, rows, wide), BF16),
            pltpu.VMEM((CUTS, rows, wide), BF16),
            pltpu.VMEM((2, 8, LANES), F32),
            pltpu.VMEM((2, modes, 8, LANES), F32),
            pltpu.VMEM((2, 8, LANES), F32),
            pltpu.VMEM((2, waves, 8, LANES), F32),
            dma((6,)),
            dma((2, CUTS)),
            dma((2, CUTS)),
            dma((2, CUTS, chips)),
            dma((2, CUTS, chips)),
            dma((2, waves)),
            dma((2, waves)),
            dma((2, waves)),
            dma((2, waves)),
            dma((chips,)),
            dma((chips,)),
            dma((chips,)),
            dma((chips,)),
            dma((2, modes)),
            dma((2, modes)),
            dma((2, waves)),
            dma((2, waves)),
        ],
        compiler_params=pltpu.CompilerParams(
            collective_id=0, has_side_effects=True, vmem_limit_bytes=56 * 1024 * 1024
        ),
        cost_estimate=pl.CostEstimate(flops=16 * count**3 * 2, bytes_accessed=12 * count**2, transcendentals=0),
    )(scales, field_in[0, 0], target[0, 0], mask_old)
    return masks[:2], masks[2:]


def chirp(scale, count):
    pos = jnp.arange(count, dtype=jnp.float32)
    diff = pos[:, None] - pos[None, :]
    angle = jnp.pi * scale * diff * diff / count
    factor = jnp.float32(count) ** (-0.5)
    return (
        (jnp.cos(angle) * factor).astype(jnp.bfloat16),
        (jnp.sin(angle) * factor).astype(jnp.bfloat16),
    )


def right_matrix(real_part, imag_part, sign):
    upper = jnp.concatenate([real_part, sign * imag_part], 1)
    lower = jnp.concatenate([-sign * imag_part, real_part], 1)
    return jnp.concatenate([upper, lower], 0)


def left_matrix(real_part, imag_part, sign):
    first = jnp.concatenate([real_part, sign * imag_part], 0)
    second = jnp.concatenate([-sign * imag_part, real_part], 0)
    return jnp.stack([first, second], 0)


def right_product(field_re, field_im, right):
    joined = jnp.concatenate([field_re, field_im], -1)
    return jnp.einsum("brk,kc->brc", joined, right, preferred_element_type=jnp.float32).astype(
        jnp.bfloat16
    )


def left_product(middle, left):
    batch = middle.shape[0]
    count = middle.shape[1]
    shaped = middle.reshape(batch, count, 2, count)
    result = jnp.einsum("pqk,bkpc->bqc", left, shaped, preferred_element_type=jnp.float32)
    return (result[:, :count], result[:, count:])


def phasor_rows(total, power_sum, count):
    power = power_sum / (count * count)
    real_part = total[:, :count]
    imag_part = total[:, count:]
    factor = lax.rsqrt(real_part * real_part + imag_part * imag_part + power + 1e-06)
    return jnp.concatenate([real_part * factor, imag_part * factor], -1).astype(jnp.bfloat16)


def as_output(mask_part, count):
    return jnp.stack([mask_part[:, :count], mask_part[:, count:]], 0)


def whole_mask(term):
    total = lax.psum(term, ("mode", "wave"))
    return phasor_rows(total, jnp.sum(total * total), term.shape[1] // 2)


def local(field_in, target, mask_old, scales):
    count = field_in.shape[-1]
    row_count = count // lax.axis_size("mode")
    kernel_re, kernel_im = chirp(scales[0], count)
    f_re = field_in[0, :, 0]
    f_im = field_in[0, :, 1]
    b_re = target[0, :, 0].astype(jnp.float32)
    b_im = target[0, :, 1].astype(jnp.float32)
    old_re = mask_old[0].astype(jnp.float32)
    old_im = mask_old[1].astype(jnp.float32)
    c_re = (b_re * old_re + b_im * old_im).astype(jnp.bfloat16)
    c_im = (b_im * old_re - b_re * old_im).astype(jnp.bfloat16)
    middle = right_product(c_re, c_im, right_matrix(kernel_re, kernel_im, -1.0))
    back_re, back_im = left_product(middle, left_matrix(kernel_re, kernel_im, -1.0))
    fr32 = f_re.astype(jnp.float32)
    fi32 = f_im.astype(jnp.float32)
    term_one = jnp.concatenate(
        [jnp.sum(back_re * fr32 + back_im * fi32, 0), jnp.sum(back_im * fr32 - back_re * fi32, 0)],
        -1,
    )
    forward_right = right_matrix(kernel_re, kernel_im, 1.0)
    mask_full = whole_mask(term_one)
    new_re = mask_full[:, :count].astype(jnp.float32)
    new_im = mask_full[:, count:].astype(jnp.float32)
    g_re = (fr32 * new_re - fi32 * new_im).astype(jnp.bfloat16)
    g_im = (fr32 * new_im + fi32 * new_re).astype(jnp.bfloat16)
    ahead_mid = right_product(g_re, g_im, forward_right)
    first_rows = lax.dynamic_slice_in_dim(
        mask_full, lax.axis_index("mode") * row_count, row_count, 0
    )
    ahead_re, ahead_im = left_product(ahead_mid, left_matrix(kernel_re, kernel_im, 1.0))
    term_two = jnp.concatenate(
        [
            jnp.sum(b_re * ahead_re + b_im * ahead_im, 0),
            jnp.sum(b_im * ahead_re - b_re * ahead_im, 0),
        ],
        -1,
    )
    second_full = whole_mask(term_two)
    second_rows = lax.dynamic_slice_in_dim(
        second_full, lax.axis_index("mode") * row_count, row_count, 0
    )
    return (as_output(first_rows, count), as_output(second_rows, count))


def solution(mesh):
    in_specs = (
        P("wave", "mode", None, None, None),
        P("wave", "mode", None, None, None),
        P(),
        P("wave"),
    )
    out_specs = (P(None, "mode", None), P(None, "mode", None))
    modes, waves = mesh.shape["mode"], mesh.shape["wave"]

    def step(field_in, target, mask_old, scales):
        count = field_in.shape[-1]
        single = field_in.shape[0] == waves and field_in.shape[1] == modes
        fits = modes % 2 == 0 and count % (modes * waves * SUB) == 0 and count % (CUTS * LANES) == 0
        body = fused if single and fits else local
        return jax.shard_map(body, mesh=mesh, in_specs=in_specs, out_specs=out_specs, check_vma=False)(
            field_in, target, mask_old, scales
        )

    return step
```

```python
import functools

import jax
import jax.numpy as jnp
from jax import lax
from jax.experimental import pallas as pl
from jax.experimental.pallas import tpu as pltpu
from jax.sharding import PartitionSpec as P

MESH = pl.DeviceIdType.MESH
F32 = jnp.float32
BF16 = jnp.bfloat16
SUB = 16
LANES = 128
CUTS = 4


def build_right(scale, right, count):
    wide = 2 * count
    half = SUB // 2
    row = lax.broadcasted_iota(jnp.int32, (half, wide), 0)
    col = lax.broadcasted_iota(jnp.int32, (half, wide), 1)
    diff = (row - col + count).astype(F32)
    angle = (jnp.pi * scale) * diff * diff / count
    factor = float(count) ** (-0.5)
    top_re = jnp.cos(angle) * factor
    top_im = jnp.sin(angle) * factor
    base_re = jnp.concatenate([top_re, pltpu.roll(top_re, half, 1)], 0)
    base_im = jnp.concatenate([top_im, pltpu.roll(top_im, half, 1)], 0)
    for shift in range(0, LANES, SUB):
        re = (pltpu.roll(base_re, shift, 1) if shift else base_re).astype(BF16)
        im = (pltpu.roll(base_im, shift, 1) if shift else base_im).astype(BF16)
        for hop in range(count // LANES):
            top = hop * LANES + shift
            begin = count - hop * LANES
            k_re = re[:, begin : begin + count]
            k_im = im[:, begin : begin + count]
            right[pl.ds(top, SUB), pl.ds(0, count)] = k_re
            right[pl.ds(top, SUB), pl.ds(count, count)] = k_im
            right[pl.ds(count + top, SUB), pl.ds(0, count)] = -k_im
            right[pl.ds(count + top, SUB), pl.ds(count, count)] = k_re


def kernel(
    modes,
    waves,
    scale_ref,
    field_hbm,
    target_hbm,
    old_hbm,
    masks,
    field,
    target,
    old,
    right,
    joined,
    middle,
    part,
    core_in,
    chip_out,
    chip_in,
    wave_out,
    wave_in,
    whole,
    last,
    power_out,
    power_in,
    power_out2,
    power_in2,
    load_s,
    core_s,
    core_r,
    chip_s,
    chip_r,
    wave_s,
    wave_r,
    gw_s,
    gw_r,
    gx_s,
    gx_r,
    gc_s,
    gc_r,
    pm_s,
    pm_r,
    pw_s,
    pw_r,
):
    count = field.shape[-1]
    chips = modes // 2
    rows = count // modes
    piece = rows // waves
    width = count // CUTS
    mode = lax.axis_index("mode")
    wave = lax.axis_index("wave")
    core = lax.rem(mode, 2)
    chip = lax.div(mode, 2)
    other = 1 - core

    loads = [
        pltpu.make_async_copy(src.at[p], dst.at[p], load_s.at[2 * i + p])
        for i, (src, dst) in enumerate(((target_hbm, target), (old_hbm, old), (field_hbm, field)))
        for p in range(2)
    ]
    for copy in loads:
        copy.start()

    barrier = pltpu.get_barrier_semaphore()
    for step in range(1, modes):
        pl.semaphore_signal(
            barrier, inc=1, device_id={"mode": lax.rem(mode + step, modes)}, device_id_type=MESH
        )
    for step in range(1, waves):
        pl.semaphore_signal(
            barrier, inc=1, device_id={"wave": lax.rem(wave + step, waves)}, device_id_type=MESH
        )

    def partner(me, size, step, turns):
        if size == 4:
            high, low = turns[step - 1]
            to = 2 * lax.rem(lax.div(me, 2) + high, 2) + lax.rem(lax.rem(me, 2) + low, 2)
            return to, to
        return lax.rem(me + step, size), lax.rem(me - step + size, size)

    chip_to = [partner(chip, chips, step, ((core, other), (other, core), (1, 1))) for step in range(1, chips)]
    other_to = [partner(chip, chips, step, ((other, core), (core, other), (1, 1))) for step in range(1, chips)]
    wave_to = [partner(wave, waves, step, ((1, 0), (1, 1), (0, 1))) for step in range(1, waves)]
    pending = []

    def send(src, dst, s_sem, r_sem, to):
        copy = pltpu.make_async_remote_copy(
            src_ref=src, dst_ref=dst, send_sem=s_sem, recv_sem=r_sem, device_id=to, device_id_type=MESH
        )
        copy.start()
        pending.append(copy)
        return copy

    def starts_of(which):
        return [pl.multiple_of((2 * q + which) * rows, rows) for q in range(chips)]

    def right_rows(low, starts, cut):
        size = rows * len(starts)
        for half, base in ((0, count), (1, 0)):
            result = jnp.dot(
                joined[pl.ds(low, size), :],
                right[:, pl.ds(half * count + cut * width, width)],
                preferred_element_type=F32,
            ).astype(BF16)
            for q, start in enumerate(starts):
                middle[pl.ds(pl.multiple_of(base + start, rows), rows), pl.ds(cut * width, width)] = result[
                    q * rows : (q + 1) * rows
                ]

    def left_half(trip, cut, which, term):
        starts = starts_of(which)
        cols = pl.ds(cut * width, width)
        lhs = jnp.concatenate(
            [right[pl.ds(s, rows), :] for s in starts]
            + [right[pl.ds(pl.multiple_of(count + s, rows), rows), :] for s in starts],
            0,
        )
        result = jnp.dot(lhs, middle[:, cols], preferred_element_type=F32)
        for q in range(chips):
            im = result[q * rows : (q + 1) * rows]
            re = result[(chips + q) * rows : (chips + q + 1) * rows]
            term_re, term_im = term(re, im, pl.ds(starts[q], rows), cols)
            part[trip, cut, which, q, :, pl.ds(0, width)] = term_re.astype(BF16)
            part[trip, cut, which, q, :, pl.ds(width, width)] = term_im.astype(BF16)

    def reduce_scatter(trip, prepare, term, ready, arrived):
        crossings = []
        for cut in range(CUTS):
            prepare(cut)
            left_half(trip, cut, other, term)
            if cut == 0:
                ready()
            crossings.append(
                send(
                    part.at[trip, cut, other],
                    core_in.at[trip, cut],
                    core_s.at[trip, cut],
                    core_r.at[trip, cut],
                    {"mode": 2 * chip + other},
                )
            )
        fans = []
        for cut in range(CUTS):
            left_half(trip, cut, core, term)
            crossings[cut].wait_recv()
            fan = []
            for step, (to, _) in enumerate(chip_to, 1):
                chip_out[trip, cut, step] = (
                    part[trip, cut, core, to].astype(F32) + core_in[trip, cut, to].astype(F32)
                ).astype(BF16)
                fan.append(
                    send(
                        chip_out.at[trip, cut, step],
                        chip_in.at[trip, cut, step],
                        chip_s.at[trip, cut, step],
                        chip_r.at[trip, cut, step],
                        {"mode": 2 * to + core},
                    )
                )
            fans.append(fan)
        hops = []
        for cut in range(CUTS):
            total = part[trip, cut, core, chip].astype(F32) + core_in[trip, cut, chip].astype(F32)
            for step, copy in enumerate(fans[cut], 1):
                copy.wait_recv()
                total = total + chip_in[trip, cut, step].astype(F32)
            wave_out[trip, cut] = total.astype(BF16).reshape(waves, piece, 2 * width)
            hop = []
            for step, (to, _) in enumerate(wave_to, 1):
                hop.append(
                    send(
                        wave_out.at[trip, cut, to],
                        wave_in.at[trip, cut, step],
                        wave_s.at[trip, cut, step],
                        wave_r.at[trip, cut, step],
                        {"wave": to},
                    )
                )
            hops.append(hop)
        for cut in range(CUTS):
            result = wave_out[trip, cut, wave].astype(F32)
            for step, copy in enumerate(hops[cut], 1):
                copy.wait_recv()
                result = result + wave_in[trip, cut, step].astype(F32)
            arrived(cut, result)

    def folded(values):
        squares = jnp.sum((values * values).reshape(piece // 8, 8, 2 * width), 0)
        tile = squares[:, :LANES]
        for low in range(LANES, 2 * width, LANES):
            tile = tile + squares[:, low : low + LANES]
        return tile

    def power_over_modes(trip, tile):
        power_out[trip] = tile
        return [
            send(
                power_out.at[trip],
                power_in.at[trip, step],
                pm_s.at[trip, step],
                pm_r.at[trip, step],
                {"mode": lax.rem(mode + step, modes)},
            )
            for step in range(1, modes)
        ]

    def power_over_waves(trip, tile, copies):
        for step, copy in enumerate(copies, 1):
            copy.wait_recv()
            tile = tile + power_in[trip, step]
        power_out2[trip] = tile
        return tile, [
            send(
                power_out2.at[trip],
                power_in2.at[trip, step],
                pw_s.at[trip, step],
                pw_r.at[trip, step],
                {"wave": lax.rem(wave + step, waves)},
            )
            for step in range(1, waves)
        ]

    def mean_power(trip, tile, copies):
        for step, copy in enumerate(copies, 1):
            copy.wait_recv()
            tile = tile + power_in2[trip, step]
        return jnp.sum(tile, keepdims=True) / (count * count)

    def phasor(block, power):
        re = block[:, :width].astype(F32)
        im = block[:, width:].astype(F32)
        factor = lax.rsqrt(re * re + im * im + power + 1e-06)
        return (re * factor).astype(BF16), (im * factor).astype(BF16)

    build_right(scale_ref[0], right, count)

    for copy in loads[:4]:
        copy.wait()
    t_re = target[0].astype(F32)
    t_im = target[1].astype(F32)
    o_re = old[0].astype(F32)
    o_im = old[1].astype(F32)
    joined[:, pl.ds(0, count)] = (t_re * o_re + t_im * o_im).astype(BF16)
    joined[:, pl.ds(count, count)] = (t_re * o_im - t_im * o_re).astype(BF16)
    every = [q * rows for q in range(modes)]

    def term_one(re, im, at, cols):
        f_re = field[0, at, cols].astype(F32)
        f_im = field[1, at, cols].astype(F32)
        return re * f_re - im * f_im, -(re * f_im + im * f_re)

    def backward_right(cut):
        right_rows(0, every, cut)
        if cut == 0:
            for copy in loads[4:]:
                copy.wait()

    def entered():
        pl.semaphore_wait(barrier, modes - 1 + waves - 1)

    mine = pl.ds(pl.multiple_of(wave * piece, piece), piece)
    squares = []
    hops = []

    def spread(trip, cut, own, value):
        own[...] = value.astype(BF16)
        hops.append(
            [
                send(
                    own,
                    own,
                    gw_s.at[trip, cut, step],
                    gw_r.at[trip, cut, step],
                    {"wave": to},
                )
                for step, (to, _) in enumerate(wave_to, 1)
            ]
        )
        squares.append(folded(value))

    reduce_scatter(
        0,
        backward_right,
        term_one,
        entered,
        lambda cut, v: spread(0, cut, whole.at[cut, core, chip, mine], v),
    )
    tile = sum(squares[1:], squares[0])
    tiles = power_over_modes(0, tile)
    fans = []
    across = []
    order = []
    for cut in range(CUTS):
        for copy in hops[cut]:
            copy.wait_recv()
        block = whole.at[cut, core, chip]
        fans.append(
            [
                send(
                    block,
                    block,
                    gx_s.at[cut, step],
                    gx_r.at[cut, step],
                    {"mode": 2 * to + core},
                )
                for step, (to, _) in enumerate(chip_to, 1)
            ]
        )
        across.append(send(block, block, gc_s.at[cut, 0], gc_r.at[cut, 0], {"mode": 2 * chip + other}))
        order.append((cut, 0))
    tile, tiles2 = power_over_waves(0, tile, tiles)
    sources = [chip] + [source for _, source in chip_to]
    others = [chip] + [source for _, source in other_to]
    for cut in range(CUTS):
        for step, copy in enumerate(fans[cut], 1):
            copy.wait_recv()
            came = whole.at[cut, core, sources[step]]
            across.append(
                send(came, came, gc_s.at[cut, step], gc_r.at[cut, step], {"mode": 2 * chip + other})
            )
            order.append((cut, step))
    power = mean_power(0, tile, tiles2)

    def masked(cut, which, source, at):
        start = pl.multiple_of((2 * source + which) * rows, rows)
        cols = pl.ds(cut * width, width)
        m_re, m_im = phasor(whole[cut, which, source], power)
        n_re = m_re.astype(F32)
        n_im = m_im.astype(F32)
        f_re = field[0, pl.ds(start, rows), cols].astype(F32)
        f_im = field[1, pl.ds(start, rows), cols].astype(F32)
        joined[at, cols] = (f_re * n_re - f_im * n_im).astype(BF16)
        joined[at, pl.ds(count + cut * width, width)] = (f_re * n_im + f_im * n_re).astype(BF16)

    def places(which, chain):
        return [pl.multiple_of((2 * source + which) * rows, rows) for source in chain]

    for step, source in enumerate(sources):
        for cut in range(CUTS):
            masked(cut, core, source, pl.ds(step * rows, rows))
    for cut in range(CUTS):
        right_rows(0, places(core, sources), cut)
    for copy, (cut, step) in zip(across, order):
        copy.wait_recv()
        masked(cut, other, others[step], pl.ds(count // 2 + step * rows, rows))

    def forward_right(cut):
        right_rows(count // 2, places(other, others), cut)

    def term_two(re, im, at, cols):
        b_re = target[0, at, cols].astype(F32)
        b_im = target[1, at, cols].astype(F32)
        return b_re * re + b_im * im, b_im * re - b_re * im

    squares.clear()
    hops.clear()
    reduce_scatter(
        1,
        forward_right,
        term_two,
        lambda: None,
        lambda cut, v: spread(1, cut, last.at[cut, mine], v),
    )
    tile = sum(squares[1:], squares[0])
    tiles = power_over_modes(1, tile)
    for cut in range(CUTS):
        cols = pl.ds(cut * width, width)
        m_re, m_im = phasor(whole[cut, core, chip], power)
        masks[0, :, cols] = m_re
        masks[1, :, cols] = m_im
    tile, tiles2 = power_over_waves(1, tile, tiles)
    for hop in hops:
        for copy in hop:
            copy.wait_recv()
    power = mean_power(1, tile, tiles2)
    for cut in range(CUTS):
        cols = pl.ds(cut * width, width)
        m_re, m_im = phasor(last[cut], power)
        masks[2, :, cols] = m_re
        masks[3, :, cols] = m_im
    for copy in pending:
        copy.wait_send()


def fused(field_in, target, mask_old, scales):
    modes = lax.axis_size("mode")
    waves = lax.axis_size("wave")
    count = field_in.shape[-1]
    chips = modes // 2
    rows = count // modes
    piece = rows // waves
    wide = 2 * count // CUTS
    dma = pltpu.SemaphoreType.DMA
    out = jax.ShapeDtypeStruct((4, rows, count), BF16)
    vmem = pl.BlockSpec(memory_space=pltpu.VMEM)
    anywhere = pl.BlockSpec(memory_space=pl.ANY)
    masks = pl.pallas_call(
        functools.partial(kernel, modes, waves),
        out_shape=out,
        in_specs=[pl.BlockSpec(memory_space=pltpu.SMEM), anywhere, anywhere, anywhere],
        out_specs=vmem,
        scratch_shapes=[
            pltpu.VMEM((2, count, count), BF16),
            pltpu.VMEM((2, count, count), BF16),
            pltpu.VMEM((2, count, count), BF16),
            pltpu.VMEM((2 * count, 2 * count), BF16),
            pltpu.VMEM((count, 2 * count), BF16),
            pltpu.VMEM((2 * count, count), BF16),
            pltpu.VMEM((2, CUTS, 2, chips, rows, wide), BF16),
            pltpu.VMEM((2, CUTS, chips, rows, wide), BF16),
            pltpu.VMEM((2, CUTS, chips, rows, wide), BF16),
            pltpu.VMEM((2, CUTS, chips, rows, wide), BF16),
            pltpu.VMEM((2, CUTS, waves, piece, wide), BF16),
            pltpu.VMEM((2, CUTS, waves, piece, wide), BF16),
            pltpu.VMEM((CUTS, 2, chips, rows, wide), BF16),
            pltpu.VMEM((CUTS, rows, wide), BF16),
            pltpu.VMEM((2, 8, LANES), F32),
            pltpu.VMEM((2, modes, 8, LANES), F32),
            pltpu.VMEM((2, 8, LANES), F32),
            pltpu.VMEM((2, waves, 8, LANES), F32),
            dma((6,)),
            dma((2, CUTS)),
            dma((2, CUTS)),
            dma((2, CUTS, chips)),
            dma((2, CUTS, chips)),
            dma((2, CUTS, waves)),
            dma((2, CUTS, waves)),
            dma((2, CUTS, waves)),
            dma((2, CUTS, waves)),
            dma((CUTS, chips)),
            dma((CUTS, chips)),
            dma((CUTS, chips)),
            dma((CUTS, chips)),
            dma((2, modes)),
            dma((2, modes)),
            dma((2, waves)),
            dma((2, waves)),
        ],
        compiler_params=pltpu.CompilerParams(
            collective_id=0, has_side_effects=True, vmem_limit_bytes=56 * 1024 * 1024
        ),
        cost_estimate=pl.CostEstimate(flops=16 * count**3 * 2, bytes_accessed=12 * count**2, transcendentals=0),
    )(scales, field_in[0, 0], target[0, 0], mask_old)
    return masks[:2], masks[2:]


def chirp(scale, count):
    pos = jnp.arange(count, dtype=jnp.float32)
    diff = pos[:, None] - pos[None, :]
    angle = jnp.pi * scale * diff * diff / count
    factor = jnp.float32(count) ** (-0.5)
    return (
        (jnp.cos(angle) * factor).astype(jnp.bfloat16),
        (jnp.sin(angle) * factor).astype(jnp.bfloat16),
    )


def right_matrix(real_part, imag_part, sign):
    upper = jnp.concatenate([real_part, sign * imag_part], 1)
    lower = jnp.concatenate([-sign * imag_part, real_part], 1)
    return jnp.concatenate([upper, lower], 0)


def left_matrix(real_part, imag_part, sign):
    first = jnp.concatenate([real_part, sign * imag_part], 0)
    second = jnp.concatenate([-sign * imag_part, real_part], 0)
    return jnp.stack([first, second], 0)


def right_product(field_re, field_im, right):
    joined = jnp.concatenate([field_re, field_im], -1)
    return jnp.einsum("brk,kc->brc", joined, right, preferred_element_type=jnp.float32).astype(
        jnp.bfloat16
    )


def left_product(middle, left):
    batch = middle.shape[0]
    count = middle.shape[1]
    shaped = middle.reshape(batch, count, 2, count)
    result = jnp.einsum("pqk,bkpc->bqc", left, shaped, preferred_element_type=jnp.float32)
    return (result[:, :count], result[:, count:])


def phasor_rows(total, power_sum, count):
    power = power_sum / (count * count)
    real_part = total[:, :count]
    imag_part = total[:, count:]
    factor = lax.rsqrt(real_part * real_part + imag_part * imag_part + power + 1e-06)
    return jnp.concatenate([real_part * factor, imag_part * factor], -1).astype(jnp.bfloat16)


def as_output(mask_part, count):
    return jnp.stack([mask_part[:, :count], mask_part[:, count:]], 0)


def whole_mask(term):
    total = lax.psum(term, ("mode", "wave"))
    return phasor_rows(total, jnp.sum(total * total), term.shape[1] // 2)


def local(field_in, target, mask_old, scales):
    count = field_in.shape[-1]
    row_count = count // lax.axis_size("mode")
    kernel_re, kernel_im = chirp(scales[0], count)
    f_re = field_in[0, :, 0]
    f_im = field_in[0, :, 1]
    b_re = target[0, :, 0].astype(jnp.float32)
    b_im = target[0, :, 1].astype(jnp.float32)
    old_re = mask_old[0].astype(jnp.float32)
    old_im = mask_old[1].astype(jnp.float32)
    c_re = (b_re * old_re + b_im * old_im).astype(jnp.bfloat16)
    c_im = (b_im * old_re - b_re * old_im).astype(jnp.bfloat16)
    middle = right_product(c_re, c_im, right_matrix(kernel_re, kernel_im, -1.0))
    back_re, back_im = left_product(middle, left_matrix(kernel_re, kernel_im, -1.0))
    fr32 = f_re.astype(jnp.float32)
    fi32 = f_im.astype(jnp.float32)
    term_one = jnp.concatenate(
        [jnp.sum(back_re * fr32 + back_im * fi32, 0), jnp.sum(back_im * fr32 - back_re * fi32, 0)],
        -1,
    )
    forward_right = right_matrix(kernel_re, kernel_im, 1.0)
    mask_full = whole_mask(term_one)
    new_re = mask_full[:, :count].astype(jnp.float32)
    new_im = mask_full[:, count:].astype(jnp.float32)
    g_re = (fr32 * new_re - fi32 * new_im).astype(jnp.bfloat16)
    g_im = (fr32 * new_im + fi32 * new_re).astype(jnp.bfloat16)
    ahead_mid = right_product(g_re, g_im, forward_right)
    first_rows = lax.dynamic_slice_in_dim(
        mask_full, lax.axis_index("mode") * row_count, row_count, 0
    )
    ahead_re, ahead_im = left_product(ahead_mid, left_matrix(kernel_re, kernel_im, 1.0))
    term_two = jnp.concatenate(
        [
            jnp.sum(b_re * ahead_re + b_im * ahead_im, 0),
            jnp.sum(b_im * ahead_re - b_re * ahead_im, 0),
        ],
        -1,
    )
    second_full = whole_mask(term_two)
    second_rows = lax.dynamic_slice_in_dim(
        second_full, lax.axis_index("mode") * row_count, row_count, 0
    )
    return (as_output(first_rows, count), as_output(second_rows, count))


def solution(mesh):
    in_specs = (
        P("wave", "mode", None, None, None),
        P("wave", "mode", None, None, None),
        P(),
        P("wave"),
    )
    out_specs = (P(None, "mode", None), P(None, "mode", None))
    modes, waves = mesh.shape["mode"], mesh.shape["wave"]

    def step(field_in, target, mask_old, scales):
        count = field_in.shape[-1]
        single = field_in.shape[0] == waves and field_in.shape[1] == modes
        fits = modes % 2 == 0 and count % (modes * waves * SUB) == 0 and count % (CUTS * LANES) == 0
        body = fused if single and fits else local
        return jax.shard_map(body, mesh=mesh, in_specs=in_specs, out_specs=out_specs, check_vma=False)(
            field_in, target, mask_old, scales
        )

    return step
```
